128 devices in a mesh: role: 2 (over x_hi), dp: 64 (over x_lo, z, y, core).
Axes of the slice: x: 4 (x_hi: 2, x_lo: 2; x = x_hi * 2 + x_lo), y: 4, z: 4, core: 2. Of those that a mesh axis runs over, the one named last changes fastest.
Arguments:
- q_start: float32 [30, 16384], P(None, ('role', 'dp')), may hold values from -3 to 3
- v_start: float32 [30, 16384], P(None, ('role', 'dp')), may hold values from -6 to 6
- minv: float32 [30, 30, 16384], P(None, None, ('role', 'dp')), as said below
- geom_jac: float32 [24, 30, 16384], P(None, None, ('role', 'dp')), may hold values from -1.75 to 1.75
- pairs: int32 [2, 48, 16384], P(None, None, ('role', 'dp')), may hold values from 0 to 23, as said below
- gap_start: float32 [48, 16384], P(None, ('role', 'dp')), may hold values from -0.05 to 0.1
- actions: int32 [8, 20, 16384], P(None, None, ('role', 'dp')), may hold values from 0 to 31
- act_map: float32 [30, 20], replicated, may hold values from -1.25 to 1.25
- batch_index: int32 [128, 128, 8], P(('role', 'dp')), may hold values from 0 to 1023
- w_in: bfloat16 [108, 1024], P(None, ('role', 'dp')), may hold values from -0.625 to 0.625
- gain_one: bfloat16 [1024], P(('role', 'dp')), may hold values from 0.5 to 1.5
- w_up: bfloat16 [1024, 2048], P(('role', 'dp')), may hold values from -0.1875 to 0.1875
- w_down: bfloat16 [2048, 1024], P(('role', 'dp')), may hold values from -0.125 to 0.125
- gain_two: bfloat16 [1024], P(('role', 'dp')), may hold values from 0.5 to 1.5
- w_head: bfloat16 [1024, 21], P(('role', 'dp')), may hold values from -0.1875 to 0.1875
- log_std: float32 [20], replicated, may hold values from 0.5 to 1.2
- old_mu: float32 [131072, 20], P(('role', 'dp')), may hold values from -6 to 6
- advantage: float32 [131072], P(('role', 'dp')), may hold values from -6 to 6
- returns: float32 [131072], P(('role', 'dp')), may hold values from -6 to 6
Outputs:
- q_final: float32 [30, 16384], P(None, ('role', 'dp'))
- v_final: float32 [30, 16384], P(None, ('role', 'dp'))
- grad_w_in: float32 [108, 1024], P(None, ('role', 'dp'))
- grad_gain_one: float32 [1024], P(('role', 'dp'))
- grad_w_up: float32 [1024, 2048], P(('role', 'dp'))
- grad_w_down: float32 [2048, 1024], P(('role', 'dp'))
- grad_gain_two: float32 [1024], P(('role', 'dp'))
- grad_w_head: float32 [1024, 21], P(('role', 'dp'))
- grad_log_std: float32 [20], replicated
- mean_loss: float32 [], replicated
The draws below stay inside these ranges and needn't reach their ends.
Inputs may be any that keep to these rules, and one draw needn't show every extreme that they name: `pairs`: the two geometries of a contact differ. `minv`: symmetric and positive definite.
All inputs are finite; a program needn't handle non-finite values.
Results may differ from the reference program's by a relative error of at most 0.02.
Values may be sent and summed in bfloat16 or wider, within the bound.
No kernel may reach another device: no remote copies, remote signals or barrier semaphores. Data moves between devices by JAX's collectives and lax.ppermute only.
A program may use at most 128 MiB of HBM per device.

```python
import math
import jax
import jax.numpy as jnp
from jax import lax

D = 1024
FF = 2048
DOF = 30
GEOMS = 24
CONT = 48
ACTS = 20
BINS = 32
STEPS = 8
ITERS = 8
ENV_DEV = 128
TOK_DEV = 1024
ENVS = 16384
TOKENS = 131072
PER_PEER = 8
OBS = 108
ROW = 128
HEADS = 21
N_ROLE = 2
N_DP = 64
DEVICES = 128


def draw_minv(key, part):
    key = jax.random.fold_in(key, 11)
    first, second = jax.random.split(key)
    scale = jnp.exp(jax.random.uniform(first, (DOF, ENVS), jnp.float32, jnp.log(0.5), jnp.log(4.0)))
    raw = jax.random.uniform(second, (DOF, DOF, ENVS), jnp.float32, -1.0, 1.0)
    sym = (raw + jnp.transpose(raw, (1, 0, 2))) * (0.45 / (DOF - 1))
    eye = jnp.eye(DOF, dtype=jnp.float32)[:, :, None]
    root = jnp.sqrt(scale)
    return root[:, None, :] * root[None, :, :] * (eye + sym * (1.0 - eye))


def draw_pairs(key, part):
    key = jax.random.fold_in(key, 12)
    first, second = jax.random.split(key)
    start = jax.random.randint(first, (CONT, ENVS), 0, GEOMS)
    offset = jax.random.randint(second, (CONT, ENVS), 1, GEOMS)
    other = (start + offset) % GEOMS
    return jnp.stack([start, other]).astype(jnp.int32)


def place_ends(entries, rng, smallest, top_value):
    dims = entries.shape
    index_at = [jax.random.randint(jax.random.fold_in(rng, axis), (), 0, dims[axis]) for axis in range(len(dims))]
    entries = entries.at[tuple(index_at)].set(smallest)
    longest = dims.index(max(dims))
    index_at[longest] = (index_at[longest] + 1) % dims[longest]
    return entries.at[tuple(index_at)].set(top_value)


def shard_levels(own_key, extent, cuts, least, largest):
    gain = 1.0
    for axis_at, shards_of in cuts:
        steps = jax.random.uniform(jax.random.fold_in(jax.random.fold_in(own_key, 6), axis_at), (shards_of,), jnp.float32, least / len(cuts), largest / len(cuts))
        gain = gain * jnp.repeat(jnp.exp(steps), extent[axis_at] // shards_of).reshape((-1,) + (1,) * (len(extent) - 1 - axis_at))
    return gain


def normal_values(stream_key, shape, deviation, bound, cuts=(), kind=jnp.bfloat16):
    array = jax.random.normal(stream_key, shape, jnp.float32) * deviation
    if len(cuts) > 0:
        array = shard_levels(stream_key, shape, cuts, -0.22, 0.18) * array
    return jnp.clip(array, min=-bound, max=bound).astype(kind)


def setup_inputs(seed: int = 0) -> dict:
    streams_of = jax.random.split(jax.random.key(seed), 20)
    q_start = normal_values(streams_of[0], (DOF, ENVS), 0.5, 3.0, ((1, 128),), jnp.float32)
    v_start = normal_values(streams_of[1], (DOF, ENVS), 1.0, 6.0, ((1, 128),), jnp.float32)
    minv = draw_minv(jax.random.fold_in(streams_of[19], 71), 0)
    geom_jac = normal_values(streams_of[3], (GEOMS, DOF, ENVS), 0.3, 1.75, ((2, 128),), jnp.float32)
    pairs = draw_pairs(jax.random.fold_in(streams_of[19], 71), 0)
    gap_start = jnp.clip(-0.05 + 0.15 * jax.random.uniform(streams_of[5], (CONT, ENVS), jnp.float32) ** shard_levels(streams_of[5], (CONT, ENVS), ((1, 128),), -0.2, 0.2), -0.05, 0.1)
    actions = place_ends(jax.random.randint(streams_of[6], (STEPS, ACTS, ENVS), 0, BINS), jax.random.fold_in(streams_of[6], 1), 0, BINS - 1).astype(jnp.int32)
    act_map = normal_values(streams_of[7], (DOF, ACTS), ACTS ** -0.5, 1.25, (), jnp.float32)
    batch_index = place_ends(jax.random.randint(streams_of[8], (DEVICES, DEVICES, PER_PEER), 0, STEPS * ENV_DEV), jax.random.fold_in(streams_of[8], 1), 0, (STEPS * ENV_DEV) - 1).astype(jnp.int32)
    w_in = normal_values(streams_of[9], (OBS, D), OBS ** -0.5, 0.625, ((1, 128),))
    gain_one = jnp.clip(1.0 + 0.1 * jax.random.normal(streams_of[10], (D,), jnp.float32), 0.5, 1.5).astype(jnp.bfloat16)
    w_up = normal_values(streams_of[11], (D, FF), D ** -0.5, 0.1875, ((0, 128),))
    w_down = normal_values(streams_of[12], (FF, D), FF ** -0.5, 0.125, ((0, 128),))
    gain_two = jnp.clip(1.0 + 0.1 * jax.random.normal(streams_of[13], (D,), jnp.float32), 0.5, 1.5).astype(jnp.bfloat16)
    w_head = normal_values(streams_of[14], (D, HEADS), D ** -0.5, 0.1875, ((0, 128),))
    log_std = jnp.clip(jax.random.uniform(streams_of[15], (ACTS,), jnp.float32, 0.5, 1.2), 0.5, 1.2)
    old_mu = normal_values(streams_of[16], (TOKENS, ACTS), 1.0, 6.0, ((0, 128),), jnp.float32)
    advantage = normal_values(streams_of[17], (TOKENS,), 1.0, 6.0, ((0, 128),), jnp.float32)
    returns = normal_values(streams_of[18], (TOKENS,), 1.0, 6.0, ((0, 128),), jnp.float32)
    return {"q_start": q_start, "v_start": v_start, "minv": minv, "geom_jac": geom_jac, "pairs": pairs, "gap_start": gap_start, "actions": actions, "act_map": act_map, "batch_index": batch_index, "w_in": w_in, "gain_one": gain_one, "w_up": w_up, "w_down": w_down, "gain_two": gain_two, "w_head": w_head, "log_std": log_std, "old_mu": old_mu, "advantage": advantage, "returns": returns}


HIGH = lax.Precision.HIGHEST
time_step = 0.02
damping = 0.5
torque = 2.0
baumgarte = 0.2
soft_reg = 0.1
clip_eps = 0.2
value_coef = 0.5
entropy_coef = 0.01
loss_scale = 1024.0

def rollout(q_start, v_start, minv, geom_jac, pairs, gap_start, actions, act_map):
    ids = jnp.arange(geom_jac.shape[0], dtype=jnp.int32)[None, :, None]
    select = (pairs[0][:, None, :] == ids).astype(jnp.float32) - (pairs[1][:, None, :] == ids).astype(jnp.float32)
    jacobian = jnp.einsum('cgb,gdb->cdb', select, geom_jac, precision=HIGH)
    mobility = jnp.einsum('dkb,ckb->dcb', minv, jacobian, precision=HIGH)
    delassus = jnp.einsum('cdb,deb->ceb', jacobian, mobility, precision=HIGH)
    denom = lax.optimization_barrier(jnp.sum(jnp.abs(delassus), axis=1)) + soft_reg

    def one_step(carry, act):
        q, v, lam = carry
        level = act.astype(jnp.float32) * (2.0 / (BINS - 1)) - 1.0
        force = torque * jnp.dot(act_map, level, precision=HIGH) - damping * v
        vfree = v + time_step * jnp.einsum('dkb,kb->db', minv, force, precision=HIGH)
        gap = gap_start + jnp.einsum('cdb,db->cb', jacobian, q - q_start, precision=HIGH)
        bias = jnp.einsum('cdb,db->cb', jacobian, vfree, precision=HIGH) + baumgarte / time_step * gap

        def sweep(index, impulse):
            push = jnp.einsum('ceb,eb->cb', delassus, impulse, precision=HIGH) + bias
            return jnp.maximum(impulse - push / denom, 0.0)
        lam = lax.fori_loop(0, ITERS, sweep, lam)
        v = vfree + jnp.einsum('dcb,cb->db', mobility, lam, precision=HIGH)
        q = q + time_step * v
        stored = jnp.concatenate([q, v, lam, level], axis=0).astype(jnp.bfloat16)
        return ((q, v, lam), stored)
    start = (q_start, v_start, jnp.zeros(gap_start.shape, jnp.float32))
    (q, v, lam), stored = lax.scan(one_step, start, actions)
    return (q, v, stored)

def normed(values):
    return values * lax.rsqrt(lax.optimization_barrier(jnp.mean(values * values, axis=-1, keepdims=True)) + 1e-05)

def partial_loss(params, rows, old_mu, advantage, returns):
    w_in, gain_one, w_up, w_down, gain_two, w_head, log_std = params
    width = w_in.shape[0]
    acts_count = log_std.shape[0]
    feats = rows[:, :width]
    taken = rows[:, width:].astype(jnp.float32)
    first = jnp.dot(feats, w_in, preferred_element_type=jnp.float32)
    norm_one = (normed(first) * gain_one.astype(jnp.float32)).astype(jnp.bfloat16)
    hidden = jax.nn.gelu(jnp.dot(norm_one, w_up, preferred_element_type=jnp.float32)).astype(jnp.bfloat16)
    second = first + jnp.dot(hidden, w_down, preferred_element_type=jnp.float32)
    norm_two = (normed(second) * gain_two.astype(jnp.float32)).astype(jnp.bfloat16)
    head = jnp.dot(norm_two, w_head, preferred_element_type=jnp.float32)
    mean = head[:, :acts_count]
    value = head[:, acts_count]
    inv_std = jnp.exp(-log_std)
    log_ratio = lax.optimization_barrier(jnp.sum(0.5 * jnp.square((taken - old_mu) * inv_std) - 0.5 * jnp.square((taken - mean) * inv_std), axis=1))
    ratio = jnp.exp(log_ratio)
    surrogate = -jnp.minimum(ratio * advantage, jnp.clip(ratio, 1.0 - clip_eps, 1.0 + clip_eps) * advantage)
    value_loss = 0.5 * jnp.square(value - returns)
    entropy = jnp.sum(log_std) + 0.5 * acts_count * (1.0 + math.log(2.0 * math.pi))
    return jnp.sum(surrogate + value_coef * value_loss - entropy_coef * entropy)

def reference(q_start, v_start, minv, geom_jac, pairs, gap_start, actions, act_map, batch_index, w_in, gain_one, w_up, w_down, gain_two, w_head, log_std, old_mu, advantage, returns):
    count = N_ROLE * N_DP
    q_final, v_final, stored = rollout(q_start, v_start, minv, geom_jac, pairs, gap_start, actions, act_map)
    buffer = stored.reshape(STEPS, ROW, count, ENV_DEV).transpose(2, 0, 3, 1).reshape(count, STEPS * ENV_DEV, ROW)
    picks = batch_index.reshape(count, count * PER_PEER)
    picked = jnp.take_along_axis(buffer, picks[:, :, None], axis=1)
    minibatch = picked.reshape(count, count, PER_PEER, ROW).transpose(1, 0, 2, 3).reshape(count, TOK_DEV, ROW)
    params = (w_in, gain_one, w_up, w_down, gain_two, w_head, log_std)
    factor = jnp.asarray(loss_scale / TOKENS, dtype=jnp.float32)

    def block(carry, pieces):
        rows_part, mu_part, adv_part, ret_part = pieces
        total, sums = carry
        value, pullback = jax.vjp(lambda p: partial_loss(p, rows_part, mu_part, adv_part, ret_part), params)
        grads = pullback(factor)[0]
        sums = tuple((s + g.astype(jnp.float32) for s, g in zip(sums, grads)))
        return ((total + value, sums), None)
    zeros = tuple((jnp.zeros(p.shape, jnp.float32) for p in params))
    pieces = (minibatch, old_mu.reshape(count, TOK_DEV, ACTS), advantage.reshape(count, TOK_DEV), returns.reshape(count, TOK_DEV))
    (total, sums), unused = lax.scan(block, (jnp.zeros((), jnp.float32), zeros), pieces)
    return (q_final, v_final, sums[0], sums[1], sums[2], sums[3], sums[4], sums[5], sums[6], total / TOKENS)
```

```python
import math

import jax
import jax.numpy as jnp
from jax import lax
from jax.sharding import Mesh
from jax.sharding import PartitionSpec as P

EVERY = ("x", "z", "y", "c")
BINS = 32
ITERS = 8


HIGH = lax.Precision.HIGHEST
time_step = 0.02
damping = 0.5
torque = 2.0
baumgarte = 0.2
soft_reg = 0.1
clip_eps = 0.2
value_coef = 0.5
entropy_coef = 0.01
loss_scale = 1024.0


def rollout(q_start, v_start, minv, geom_jac, pairs, gap_start, actions, act_map):
    ids = jnp.arange(geom_jac.shape[0], dtype=jnp.int32)[None, :, None]
    select = (pairs[0][:, None, :] == ids).astype(jnp.float32) - (
        pairs[1][:, None, :] == ids
    ).astype(jnp.float32)
    jacobian = jnp.einsum("cgb,gdb->cdb", select, geom_jac, precision=HIGH)
    mobility = jnp.einsum("dkb,ckb->dcb", minv, jacobian, precision=HIGH)
    delassus = jnp.einsum("cdb,deb->ceb", jacobian, mobility, precision=HIGH)
    denom = jnp.sum(jnp.abs(delassus), axis=1) + soft_reg

    def one_step(carry, act):
        q, v, lam = carry
        level = act.astype(jnp.float32) * (2.0 / (BINS - 1)) - 1.0
        force = torque * jnp.dot(act_map, level, precision=HIGH) - damping * v
        vfree = v + time_step * jnp.einsum("dkb,kb->db", minv, force, precision=HIGH)
        gap = gap_start + jnp.einsum("cdb,db->cb", jacobian, q - q_start, precision=HIGH)
        bias = (
            jnp.einsum("cdb,db->cb", jacobian, vfree, precision=HIGH) + baumgarte / time_step * gap
        )

        def sweep(index, impulse):
            push = jnp.einsum("ceb,eb->cb", delassus, impulse, precision=HIGH) + bias
            return jnp.maximum(impulse - push / denom, 0.0)

        lam = lax.fori_loop(0, ITERS, sweep, lam)
        v = vfree + jnp.einsum("dcb,cb->db", mobility, lam, precision=HIGH)
        q = q + time_step * v
        stored = jnp.concatenate([q, v, lam, level], axis=0).astype(jnp.bfloat16)
        return ((q, v, lam), stored)

    start = (q_start, v_start, jnp.zeros(gap_start.shape, jnp.float32))
    (q, v, lam), stored = lax.scan(one_step, start, actions)
    return (q, v, stored)


def normed(values):
    return values * lax.rsqrt(jnp.mean(values * values, axis=-1, keepdims=True) + 1e-05)


def partial_loss(params, rows, old_mu, advantage, returns):
    w_in, gain_one, w_up, w_down, gain_two, w_head, log_std = params
    width = w_in.shape[0]
    acts_count = log_std.shape[0]
    feats = rows[:, :width]
    taken = rows[:, width:].astype(jnp.float32)
    first = jnp.dot(feats, w_in, preferred_element_type=jnp.float32)
    norm_one = (normed(first) * gain_one.astype(jnp.float32)).astype(jnp.bfloat16)
    hidden = jax.nn.gelu(jnp.dot(norm_one, w_up, preferred_element_type=jnp.float32)).astype(
        jnp.bfloat16
    )
    second = first + jnp.dot(hidden, w_down, preferred_element_type=jnp.float32)
    norm_two = (normed(second) * gain_two.astype(jnp.float32)).astype(jnp.bfloat16)
    head = jnp.dot(norm_two, w_head, preferred_element_type=jnp.float32)
    mean = head[:, :acts_count]
    value = head[:, acts_count]
    inv_std = jnp.exp(-log_std)
    log_ratio = jnp.sum(
        0.5 * jnp.square((taken - old_mu) * inv_std) - 0.5 * jnp.square((taken - mean) * inv_std),
        axis=1,
    )
    ratio = jnp.exp(log_ratio)
    surrogate = -jnp.minimum(
        ratio * advantage, jnp.clip(ratio, 1.0 - clip_eps, 1.0 + clip_eps) * advantage
    )
    value_loss = 0.5 * jnp.square(value - returns)
    entropy = jnp.sum(log_std) + 0.5 * acts_count * (1.0 + math.log(2.0 * math.pi))
    return jnp.sum(surrogate + value_coef * value_loss - entropy_coef * entropy)


WIRE = ("x", "z", "y")
SMALL = 256


def pieces_of(values):
    first = lax.reduce_precision(values, 8, 7)
    second = lax.reduce_precision(values - first, 8, 7)
    third = values - first - second
    return jnp.concatenate([first, second, third], axis=-1).astype(jnp.bfloat16)


def pair_sum(grad):
    core = lax.axis_index("c")
    other = lax.dynamic_index_in_dim(grad, 1 - core, axis=1, keepdims=False)
    own = lax.dynamic_index_in_dim(grad, core, axis=1, keepdims=False)
    came = lax.ppermute(other, "c", [(0, 1), (1, 0)])
    return (own.astype(jnp.float32) + came.astype(jnp.float32)).astype(jnp.bfloat16)


def body(
    q_start,
    v_start,
    minv,
    geom_jac,
    pairs,
    gap_start,
    actions,
    act_map,
    batch_index,
    w_in,
    gain_one,
    w_up,
    w_down,
    gain_two,
    w_head,
    log_std,
    old_mu,
    advantage,
    returns,
):
    count = lax.axis_size(EVERY)
    chips = count // 2
    rows_up, ff = w_up.shape
    rows_down, width = w_down.shape
    obs = w_in.shape[0]
    heads = w_head.shape[1]
    filled = obs + heads + 2
    small = jnp.concatenate(
        [
            jnp.transpose(w_in),
            w_head,
            gain_one[:, None],
            gain_two[:, None],
            jnp.zeros((rows_up, SMALL - filled), jnp.bfloat16),
        ],
        axis=1,
    )
    packed = jnp.concatenate([w_up, w_down[:rows_up], w_down[rows_up:], small], axis=1)
    weights = lax.all_gather(packed, EVERY, axis=0, tiled=True)

    q_final, v_final, stored = rollout(
        q_start, v_start, minv, geom_jac, pairs, gap_start, actions, act_map
    )
    per_peer = batch_index.shape[2]
    row_width = stored.shape[1]
    flat = jnp.transpose(stored, (0, 2, 1)).reshape(-1, row_width)
    picked = jnp.take(flat, batch_index[0].reshape(-1), axis=0).reshape(count, per_peer, row_width)
    arrived = lax.all_to_all(picked, EVERY, split_axis=0, concat_axis=0, tiled=True)
    rows = arrived.reshape(-1, row_width)

    up = weights[:, :ff]
    down = (
        weights[:, ff : ff + 2 * width]
        .reshape(count, rows_up, 2, width)
        .transpose(0, 2, 1, 3)
        .reshape(count * rows_down, width)
    )
    rest = weights[:, ff + 2 * width :]
    params = (
        jnp.transpose(rest[:, :obs]),
        rest[:, obs + heads],
        up,
        down,
        rest[:, obs + heads + 1],
        rest[:, obs : obs + heads],
        log_std,
    )
    factor = jnp.asarray(loss_scale / (rows.shape[0] * count), dtype=jnp.float32)
    partial_value, pullback = jax.vjp(
        lambda p: partial_loss(p, rows, old_mu, advantage, returns), params
    )
    grads = pullback(factor)[0]

    down_pair = pair_sum(grads[3].reshape(chips, 2, rows_down, width))
    down_came = lax.all_to_all(down_pair, WIRE, split_axis=0, concat_axis=0, tiled=True)
    grad_down = jnp.sum(down_came.astype(jnp.float32), axis=0)

    totals = jnp.concatenate([grads[6], partial_value[None]])
    totals = totals + lax.ppermute(totals, "c", [(0, 1), (1, 0)])
    n_totals = totals.shape[0]
    grad_small = jnp.concatenate(
        [
            jnp.transpose(grads[0]),
            grads[5],
            grads[1][:, None],
            grads[4][:, None],
            jnp.zeros((count * rows_up, SMALL - filled), jnp.bfloat16),
        ],
        axis=1,
    )
    up_pair = pair_sum(
        jnp.concatenate([grads[2], grad_small], axis=1).reshape(chips, 2, rows_up, ff + SMALL)
    )
    place = ff + filled
    up_pair = up_pair.at[:, 0, place : place + 3 * n_totals].set(pieces_of(totals)[None])
    up_came = lax.all_to_all(up_pair, WIRE, split_axis=0, concat_axis=0, tiled=True)
    summed = jnp.sum(up_came.astype(jnp.float32), axis=0)
    grad_up = summed[:, :ff]
    tail = summed[:, ff:]
    whole = tail[0, filled : filled + 3 * n_totals].reshape(3, n_totals).sum(axis=0)
    mean_loss = whole[n_totals - 1] / (rows.shape[0] * count)
    return (
        q_final,
        v_final,
        jnp.transpose(tail[:, :obs]),
        tail[:, obs + heads],
        grad_up,
        grad_down,
        tail[:, obs + heads + 1],
        tail[:, obs : obs + heads],
        whole[: n_totals - 1],
        mean_loss,
    )


def solution(mesh):
    grid = Mesh(mesh.devices.reshape(4, 4, 4, 2), EVERY)
    placed = (
        P(None, EVERY),
        P(None, EVERY),
        P(None, None, EVERY),
        P(None, None, EVERY),
        P(None, None, EVERY),
        P(None, EVERY),
        P(None, None, EVERY),
        P(),
        P(EVERY, None, None),
        P(None, EVERY),
        P(EVERY),
        P(EVERY, None),
        P(EVERY, None),
        P(EVERY),
        P(EVERY, None),
        P(),
        P(EVERY, None),
        P(EVERY),
        P(EVERY),
    )
    return jax.shard_map(
        body,
        mesh=grid,
        in_specs=placed,
        out_specs=(
            P(None, EVERY),
            P(None, EVERY),
            P(None, EVERY),
            P(EVERY),
            P(EVERY, None),
            P(EVERY, None),
            P(EVERY),
            P(EVERY, None),
            P(),
            P(),
        ),
        check_vma=False,
    )
```

```python
import math

import jax
import jax.numpy as jnp
from jax import lax
from jax.experimental import pallas as pl
from jax.experimental.pallas import tpu as pltpu
from jax.sharding import Mesh
from jax.sharding import PartitionSpec as P

EVERY = ("x", "z", "y", "c")
WIRE = ("x", "z", "y")
LANES = 128
SWAP = [(0, 1), (1, 0)]
VMEM_LIMIT = 58 * 1024 * 1024

BINS = 32
ITERS = 8
time_step = 0.02
damping = 0.5
torque = 2.0
baumgarte = 0.2
soft_reg = 0.1
clip_eps = 0.2
value_coef = 0.5
entropy_coef = 0.01
loss_scale = 1024.0

VMEM = pl.BlockSpec(memory_space=pltpu.VMEM)
SMEM = pl.BlockSpec(memory_space=pltpu.SMEM)


def dot(a, b, dims, precision=None):
    return lax.dot_general(
        a, b, (dims, ((), ())), precision=precision, preferred_element_type=jnp.float32
    )


NN = ((1,), (0,))
NT = ((1,), (1,))
TN = ((0,), (0,))


def spread(row, rows):
    return jnp.broadcast_to(row, (rows, row.shape[-1]))


def rollout_kernel(
    q_ref, v_ref, minv_ref, geom_ref, pairs_ref, gap_ref, act_ref, map_ref, picks_ref,
    q_out, v_out, rows_out,
    select, jac, mob, dela, stored,
):
    geoms, dof, envs = geom_ref.shape
    cont = gap_ref.shape[0]
    steps, acts, _ = act_ref.shape

    @pl.loop(0, geoms)
    def _(g):
        first = (pairs_ref[0] == g).astype(jnp.float32)
        select[g] = first - (pairs_ref[1] == g).astype(jnp.float32)

    def by_rows(count, many, depth, left, right, out):
        @pl.loop(0, count // many)
        def _(block):
            sums = [jnp.zeros((cont, envs), jnp.float32) for _ in range(many)]
            for k in range(depth):
                held = right(k)
                for i in range(many):
                    sums[i] = sums[i] + spread(left(k, block * many + i), cont) * held
            for i in range(many):
                out[block * many + i] = sums[i]

    by_rows(dof, 3, geoms, lambda g, d: geom_ref[g, pl.ds(d, 1), :], lambda g: select[g], jac)
    by_rows(dof, 3, dof, lambda k, d: minv_ref[d, pl.ds(k, 1), :], lambda k: jac[k], mob)
    by_rows(cont, 4, dof, lambda d, e: mob[d, pl.ds(e, 1), :], lambda d: jac[d], dela)

    denom = jnp.full((cont, envs), soft_reg, jnp.float32)
    for e in range(cont):
        denom = denom + jnp.abs(dela[e])
    inverse = 1.0 / denom
    gap_rate = baumgarte / time_step
    q_first = q_ref[...]
    gap_first = gap_ref[...] * gap_rate

    def one_step(s, carry):
        q, v, lam = carry
        level = act_ref[s].astype(jnp.float32) * (2.0 / (BINS - 1)) - 1.0
        force = torque * dot(map_ref[...], level, NN, lax.Precision.HIGHEST) - damping * v
        pushed = jnp.zeros_like(v)
        for k in range(dof):
            pushed = pushed + minv_ref[k] * spread(force[k : k + 1], dof)
        vfree = v + time_step * pushed
        drift = vfree + gap_rate * (q - q_first)
        bias = gap_first
        for d in range(dof):
            bias = bias + jac[d] * spread(drift[d : d + 1], cont)

        def sweep(_, lam):
            push = [bias, jnp.zeros_like(bias)]
            for e in range(cont):
                push[e % 2] = push[e % 2] + dela[e] * spread(lam[e : e + 1], cont)
            return jnp.maximum(lam - (push[0] + push[1]) * inverse, 0.0)

        lam = lax.fori_loop(0, ITERS, sweep, lam)
        gained = [jnp.sum(mob[d] * lam, axis=0, keepdims=True) for d in range(dof)]
        v = vfree + jnp.concatenate(gained, axis=0)
        q = q + time_step * v
        stored[s] = jnp.concatenate([q, v, lam, level], axis=0).astype(jnp.bfloat16)
        return q, v, lam

    q, v, _ = lax.fori_loop(
        0, steps, one_step, (q_first, v_ref[...], jnp.zeros((cont, envs), jnp.float32))
    )
    q_out[...] = q
    v_out[...] = v

    picks = picks_ref.shape[1]
    block = 256
    for start in range(0, picks, block):
        wanted = picks_ref[:, start : start + block]
        found = jnp.zeros((stored.shape[1], block), jnp.float32)
        for s in range(steps):
            ids = lax.broadcasted_iota(jnp.int32, (envs, block), 0) + s * envs
            hit = (ids == wanted).astype(jnp.float32).astype(jnp.bfloat16)
            found = found + dot(stored[s], hit, NN)
        rows_out[start : start + block, :] = jnp.transpose(found).astype(jnp.bfloat16)


def rollout(q_start, v_start, minv, geom_jac, pairs, gap_start, actions, act_map, picks):
    geoms, dof, envs = geom_jac.shape
    cont = gap_start.shape[0]
    steps, acts, _ = actions.shape
    row = 2 * dof + cont + acts
    return pl.pallas_call(
        rollout_kernel,
        out_shape=(
            jax.ShapeDtypeStruct((dof, envs), jnp.float32),
            jax.ShapeDtypeStruct((dof, envs), jnp.float32),
            jax.ShapeDtypeStruct((picks.shape[1], row), jnp.bfloat16),
        ),
        in_specs=[VMEM] * 9,
        out_specs=(VMEM,) * 3,
        scratch_shapes=[
            pltpu.VMEM((geoms, cont, envs), jnp.float32),
            pltpu.VMEM((dof, cont, envs), jnp.float32),
            pltpu.VMEM((dof, cont, envs), jnp.float32),
            pltpu.VMEM((cont, cont, envs), jnp.float32),
            pltpu.VMEM((steps, row, envs), jnp.bfloat16),
        ],
        compiler_params=pltpu.CompilerParams(vmem_limit_bytes=VMEM_LIMIT),
        name="rollout",
    )(q_start, v_start, minv, geom_jac, pairs, gap_start, actions, act_map, picks)


TOKEN_BLOCK = 512
HBM = pl.BlockSpec(memory_space=pl.ANY)
GELU_RATE = math.sqrt(2.0 / math.pi)
GELU_CUBE = 0.044715 * GELU_RATE


def mean_square_root(values):
    return lax.rsqrt(jnp.mean(values * values, axis=1, keepdims=True) + 1e-05)


def norm_backward(grad, values, root):
    inner = jnp.mean(grad * values, axis=1, keepdims=True)
    return root * (grad - values * (root * root * inner))


def split_by_core(core, block, rows, keep_ref, send_ref, start, lane):
    count, columns = block.shape
    groups = block.reshape(count // (2 * rows), 2, rows, columns)
    half = count // 2
    at = pl.ds(pl.multiple_of(start, half), half)
    lanes = slice(lane, lane + columns)
    for which in range(2):
        part = groups[:, which].reshape(half, columns).astype(jnp.bfloat16)

        @pl.when(core == which)
        def _():
            keep_ref[at, lanes] = part

        @pl.when(core != which)
        def _():
            send_ref[at, lanes] = part


def pack_kernel(up_ref, down_ref, in_ref, head_ref, gains_ref, out_ref):
    rows, ff = up_ref.shape
    width = down_ref.shape[1]
    obs = in_ref.shape[0]
    heads = head_ref.shape[1]
    out_ref[:, :ff] = up_ref[...]
    down = down_ref[...].astype(jnp.float32)
    out_ref[:, ff : ff + width] = down[:rows].astype(jnp.bfloat16)
    out_ref[:, ff + width : ff + 2 * width] = down[rows:].astype(jnp.bfloat16)
    first = jnp.concatenate(
        [in_ref[...].astype(jnp.float32), jnp.zeros((LANES - obs, rows), jnp.float32)], axis=0
    )
    gains = jnp.concatenate(
        [gains_ref[...].astype(jnp.float32), jnp.zeros((LANES - 2, rows), jnp.float32)], axis=0
    )
    second = pltpu.roll(jnp.transpose(gains), heads, 1)
    wide = jnp.concatenate(
        [head_ref[...].astype(jnp.float32), jnp.zeros((rows, LANES - heads), jnp.float32)], axis=1
    )
    both = jnp.concatenate([jnp.transpose(first), second + wide], axis=1)
    out_ref[:, ff + 2 * width :] = both.astype(jnp.bfloat16)


def pack(w_up, w_down, w_in, w_head, gains):
    rows, ff = w_up.shape
    width = w_down.shape[1]
    return pl.pallas_call(
        pack_kernel,
        out_shape=jax.ShapeDtypeStruct((rows, ff + 2 * width + 2 * LANES), jnp.bfloat16),
        in_specs=[VMEM] * 5,
        out_specs=VMEM,
        name="pack",
    )(w_up, w_down, w_in, w_head, gains)


def columns_in(weights_ref, parts, start, out_ref, sem):
    rows, total = weights_ref.shape
    columns = out_ref.shape[1]
    each = total // parts
    return [
        pltpu.make_async_copy(
            weights_ref.at[:, pl.ds(part * each + start, columns)],
            out_ref.at[pl.ds(part * rows, rows), :],
            sem.at[part],
        )
        for part in range(parts)
    ]


def forward_kernel(
    acts, factor, parts,
    core_ref, rows_ref, aux_ref, std_ref, weights_ref,
    keep_hbm, send_hbm, pre_hbm, dsecond_hbm, norm_hbm, down_hbm, dhead_ref, totals_ref, gains_ref,
    up_ref, both_ref, small_ref, down_ref, hidden_ref, pre_ref, dsecond_ref, norm_ref, keep_ref, send_ref,
    in_sem, out_sem,
):
    tokens = rows_ref.shape[0]
    width, ff = up_ref.shape
    load_small = columns_in(weights_ref, parts, ff + 2 * width, small_ref, in_sem.at[0])
    load_up = columns_in(weights_ref, parts, 0, up_ref, in_sem.at[1])
    load_both = columns_in(weights_ref, parts, ff, both_ref, in_sem.at[2])
    for copy in load_small + load_both + load_up:
        copy.start()

    inv_std = jnp.exp(-std_ref[...])
    lane = lax.broadcasted_iota(jnp.int32, (1, LANES), 1)
    is_act = lane < acts
    entropy = jnp.sum(jnp.where(is_act, std_ref[...], 0.0)) + 0.5 * acts * (
        1.0 + math.log(2.0 * math.pi)
    )
    dhead_ref[...] = jnp.zeros_like(dhead_ref)
    totals_ref[...] = jnp.zeros_like(totals_ref)
    low, high = 1.0 - clip_eps, 1.0 + clip_eps

    for copy in load_small:
        copy.wait()
    gains_ref[...] = jnp.transpose(small_ref[:, LANES:].astype(jnp.float32))[acts + 1 : acts + 9]
    gain_one = gains_ref[0:1, :]
    gain_two = gains_ref[1:2, :]

    many = 128
    for part, copy in enumerate(load_both):
        copy.wait()

        @pl.loop(part * (width // parts) // many, (part + 1) * (width // parts) // many)
        def _(block):
            at = pl.ds(pl.multiple_of(block * many, many), many)
            halves = both_ref[at, :].astype(jnp.float32).reshape(many // 8, 8, 2 * width)
            mixed = jnp.stack([halves[:, :, :width], halves[:, :, width:]], axis=1)
            to = pl.ds(pl.multiple_of(block * 2 * many, 2 * many), 2 * many)
            down_ref[to, :] = mixed.reshape(2 * many, width).astype(jnp.bfloat16)

    down_out = pltpu.make_async_copy(down_ref, down_hbm, out_sem.at[0])
    down_out.start()
    for copy in load_up:
        copy.wait()

    @pl.loop(0, tokens // TOKEN_BLOCK)
    def _(block):
        at = pl.ds(pl.multiple_of(block * TOKEN_BLOCK, TOKEN_BLOCK), TOKEN_BLOCK)
        rows = rows_ref[at, :]
        first = dot(rows, small_ref[:, :LANES], NT)
        norm_one = (first * mean_square_root(first) * gain_one).astype(jnp.bfloat16)
        norm_ref[at, :] = norm_one
        second = first
        chunk = 512
        for start in range(0, ff, chunk):
            lanes = slice(start, start + chunk)
            pre = dot(norm_one, up_ref[:, lanes], NN)
            pre_ref[at, lanes] = pre.astype(jnp.bfloat16)
            bent = jnp.tanh(pre * (GELU_RATE + GELU_CUBE * (pre * pre)))
            half = 0.5 * pre
            hidden = (half + half * bent).astype(jnp.bfloat16)
            hidden_ref[at, lanes] = hidden
            second = second + dot(hidden, down_ref[lanes, :], NN)
        pltpu.make_async_copy(pre_ref.at[at, :], pre_hbm.at[at, :], out_sem.at[1]).start()
        pltpu.make_async_copy(norm_ref.at[at, :], norm_hbm.at[at, :], out_sem.at[2]).start()
        root_two = mean_square_root(second)
        scaled = second * root_two
        norm_two = (scaled * gain_two).astype(jnp.bfloat16)
        head = dot(norm_two, small_ref[:, LANES:], NN)

        aux = aux_ref[at, :]
        advantage = aux[:, acts : acts + 1]
        returns = aux[:, acts + 1 : acts + 2]
        taken = pltpu.roll(rows.astype(jnp.float32), acts, 1)
        from_old = jnp.where(is_act, (taken - aux) * inv_std, 0.0)
        from_new = jnp.where(is_act, (taken - head) * inv_std, 0.0)
        apart = from_old * from_old - from_new * from_new
        ratio = jnp.exp(0.5 * jnp.sum(apart, axis=1, keepdims=True))
        free = ratio * advantage
        held = jnp.clip(ratio, low, high) * advantage
        missed = head[:, acts : acts + 1] - returns
        losses = (
            -jnp.minimum(free, held)
            + (0.5 * value_coef) * missed * missed
            - entropy_coef * entropy
        )
        on_free = jnp.where(free < held, 1.0, jnp.where(free == held, 0.5, 0.0))
        inside = jnp.where(
            (ratio > low) & (ratio < high),
            1.0,
            jnp.where((ratio == low) | (ratio == high), 0.5, 0.0),
        )
        dratio = -advantage * (on_free + (1.0 - on_free) * inside)
        dlog = (factor * dratio) * ratio
        dhead = jnp.where(
            is_act,
            dlog * (from_new * inv_std),
            jnp.where(lane == acts, (factor * value_coef) * missed, 0.0),
        )
        dstd = jnp.where(is_act, -dlog * apart - factor * entropy_coef, 0.0)
        both = jnp.where(lane == acts, losses, dstd)
        totals_ref[...] += jnp.sum(both, axis=0, keepdims=True)

        dhead = dhead.astype(jnp.bfloat16)
        dnorm = dot(dhead, small_ref[:, LANES:], NT)
        dhead_ref[0:LANES, :] += dot(dhead, norm_two, TN)
        dhead_ref[LANES : LANES + 1, :] += jnp.sum(dnorm * scaled, axis=0, keepdims=True)
        dsecond = norm_backward(dnorm * gain_two, second, root_two)
        dsecond_ref[at, :] = dsecond.astype(jnp.bfloat16)
        pltpu.make_async_copy(dsecond_ref.at[at, :], dsecond_hbm.at[at, :], out_sem.at[3]).start()

    chunk = 256

    @pl.loop(0, ff // chunk)
    def _(block):
        lanes = pl.ds(pl.multiple_of(block * chunk, chunk), chunk)
        grad = dot(hidden_ref[:, lanes], dsecond_ref[...], TN)
        start = block * (chunk // 2)
        split_by_core(core_ref[0], grad, 16, keep_ref, send_ref, start, 0)
        at = pl.ds(pl.multiple_of(start, chunk // 2), chunk // 2)
        pltpu.make_async_copy(keep_ref.at[at, :], keep_hbm.at[at, :], out_sem.at[4]).start()
        pltpu.make_async_copy(send_ref.at[at, :], send_hbm.at[at, :], out_sem.at[5]).start()

    down_out.wait()
    outs = ((pre_ref, pre_hbm), (norm_ref, norm_hbm), (dsecond_ref, dsecond_hbm))
    for place, (here, there) in enumerate(outs + ((keep_ref, keep_hbm), (send_ref, send_hbm))):
        pltpu.make_async_copy(here, there, out_sem.at[place + 1]).wait()


def forward(core, rows, aux, std, weights, ff, acts, factor):
    tokens = rows.shape[0]
    group, total = weights.shape
    width = 1024
    parts = width // group
    bf16, f32 = jnp.bfloat16, jnp.float32
    shapes = [(ff // 2, width), (ff // 2, width), (tokens, ff), (tokens, width), (tokens, width), (ff, width)]
    return pl.pallas_call(
        lambda *refs: forward_kernel(acts, factor, parts, *refs),
        out_shape=tuple(jax.ShapeDtypeStruct(shape, bf16) for shape in shapes)
        + (
            jax.ShapeDtypeStruct((LANES + 8, width), f32),
            jax.ShapeDtypeStruct((1, LANES), f32),
            jax.ShapeDtypeStruct((8, width), f32),
        ),
        in_specs=[SMEM] + [VMEM] * 3 + [HBM],
        out_specs=(HBM,) * 6 + (VMEM,) * 3,
        scratch_shapes=[
            pltpu.VMEM((width, ff), bf16),
            pltpu.VMEM((width, 2 * width), bf16),
            pltpu.VMEM((width, 2 * LANES), bf16),
            pltpu.VMEM((ff, width), bf16),
            pltpu.VMEM((tokens, ff), bf16),
            pltpu.VMEM((tokens, ff), bf16),
            pltpu.VMEM((tokens, width), bf16),
            pltpu.VMEM((tokens, width), bf16),
            pltpu.VMEM((ff // 2, width), bf16),
            pltpu.VMEM((ff // 2, width), bf16),
            pltpu.SemaphoreType.DMA((3, parts)),
            pltpu.SemaphoreType.DMA((6,)),
        ],
        compiler_params=pltpu.CompilerParams(vmem_limit_bytes=VMEM_LIMIT),
        cost_estimate=pl.CostEstimate(
            flops=6 * tokens * width * ff, bytes_accessed=30 << 20, transcendentals=tokens * ff
        ),
        name="forward",
    )(core, rows, aux, std, weights)


def backward_kernel(
    heads, parts,
    core_ref, rows_ref, weights_ref, gains_ref, pre_hbm, dsecond_hbm, norm_hbm, down_hbm, dhead_ref,
    keep_hbm, send_hbm,
    up_ref, win_ref, down_ref, pre_ref, dsecond_ref, norm_ref, dpre_ref, din_ref, dgain_ref, keep_ref, send_ref,
    in_sem, out_sem,
):
    tokens = rows_ref.shape[0]
    width, ff = up_ref.shape
    load_win = columns_in(weights_ref, parts, ff + 2 * width, win_ref, in_sem.at[0])
    load_up = columns_in(weights_ref, parts, 0, up_ref, in_sem.at[1])
    pairs = ((dsecond_hbm, dsecond_ref), (down_hbm, down_ref), (pre_hbm, pre_ref), (norm_hbm, norm_ref))
    loads = [
        pltpu.make_async_copy(there, here, in_sem.at[2, place])
        for place, (there, here) in enumerate(pairs)
    ]
    for copy in load_win + loads[:3] + load_up + loads[3:]:
        copy.start()
    gain_one = gains_ref[0:1, :]
    din_ref[...] = jnp.zeros_like(din_ref)
    dgain_ref[...] = jnp.zeros_like(dgain_ref)
    for copy in load_win + loads[:3] + load_up:
        copy.wait()

    @pl.loop(0, tokens // TOKEN_BLOCK)
    def _(block):
        at = pl.ds(pl.multiple_of(block * TOKEN_BLOCK, TOKEN_BLOCK), TOKEN_BLOCK)
        rows = rows_ref[at, :]
        first = dot(rows, win_ref[...], NT)
        root = mean_square_root(first)
        dsecond = dsecond_ref[at, :]
        dnorm = jnp.zeros((TOKEN_BLOCK, width), jnp.float32)
        chunk = 512
        for start in range(0, ff, chunk):
            lanes = slice(start, start + chunk)
            dhidden = dot(dsecond, down_ref[lanes, :], NT)
            pre = pre_ref[at, lanes].astype(jnp.float32)
            square = pre * pre
            bent = jnp.tanh(pre * (GELU_RATE + GELU_CUBE * square))
            half = 0.5 * pre
            slope = 0.5 + 0.5 * bent + (half - half * (bent * bent)) * (
                GELU_RATE + (3.0 * GELU_CUBE) * square
            )
            dpre = (dhidden * slope).astype(jnp.bfloat16)
            dpre_ref[at, lanes] = dpre
            dnorm = dnorm + dot(dpre, up_ref[:, lanes], NT)
        dgain_ref[0:1, :] += jnp.sum(dnorm * (first * root), axis=0, keepdims=True)
        dfirst = dsecond.astype(jnp.float32) + norm_backward(dnorm * gain_one, first, root)
        din_ref[...] += dot(rows, dfirst.astype(jnp.bfloat16), TN)

    loads[3].wait()
    chunk = 256
    ids = lax.broadcasted_iota(jnp.int32, (LANES, chunk), 0)

    @pl.loop(0, width // chunk)
    def _(block):
        lanes = pl.ds(pl.multiple_of(block * chunk, chunk), chunk)
        core = core_ref[0]
        half = block * (chunk // 2)
        for start in range(0, ff, 1024):
            grad = dot(norm_ref[:, lanes], dpre_ref[:, start : start + 1024], TN)
            split_by_core(core, grad, 8, keep_ref, send_ref, half, start)
        split_by_core(core, jnp.transpose(din_ref[:, lanes]), 8, keep_ref, send_ref, half, ff)
        tail = jnp.where(ids == heads, dgain_ref[0:1, lanes], dhead_ref[0:LANES, lanes])
        tail = jnp.where(ids == heads + 1, dhead_ref[LANES : LANES + 1, lanes], tail)
        split_by_core(core, jnp.transpose(tail), 8, keep_ref, send_ref, half, ff + LANES)
        at = pl.ds(pl.multiple_of(half, chunk // 2), chunk // 2)
        pltpu.make_async_copy(keep_ref.at[at, :], keep_hbm.at[at, :], out_sem.at[0]).start()
        pltpu.make_async_copy(send_ref.at[at, :], send_hbm.at[at, :], out_sem.at[1]).start()

    pltpu.make_async_copy(keep_ref, keep_hbm, out_sem.at[0]).wait()
    pltpu.make_async_copy(send_ref, send_hbm, out_sem.at[1]).wait()


def backward(heads, core, rows, weights, gains, pre, dsecond, norm_one, down, dhead):
    tokens, ff = pre.shape
    width = dsecond.shape[1]
    parts = width // weights.shape[0]
    bf16, f32 = jnp.bfloat16, jnp.float32
    out = jax.ShapeDtypeStruct((width // 2, ff + 2 * LANES), bf16)
    return pl.pallas_call(
        lambda *refs: backward_kernel(heads, parts, *refs),
        out_shape=(out, out),
        in_specs=[SMEM, VMEM, HBM, VMEM] + [HBM] * 4 + [VMEM],
        out_specs=(HBM, HBM),
        scratch_shapes=[
            pltpu.VMEM((width, ff), bf16),
            pltpu.VMEM((width, LANES), bf16),
            pltpu.VMEM((ff, width), bf16),
            pltpu.VMEM((tokens, ff), bf16),
            pltpu.VMEM((tokens, width), bf16),
            pltpu.VMEM((tokens, width), bf16),
            pltpu.VMEM((tokens, ff), bf16),
            pltpu.VMEM((LANES, width), f32),
            pltpu.VMEM((8, width), f32),
            pltpu.VMEM(out.shape, bf16),
            pltpu.VMEM(out.shape, bf16),
            pltpu.SemaphoreType.DMA((3, max(parts, 4))),
            pltpu.SemaphoreType.DMA((2,)),
        ],
        compiler_params=pltpu.CompilerParams(vmem_limit_bytes=VMEM_LIMIT),
        cost_estimate=pl.CostEstimate(
            flops=6 * tokens * width * ff, bytes_accessed=30 << 20, transcendentals=tokens * ff
        ),
        name="backward",
    )(core, rows, weights, gains, pre, dsecond, norm_one, down, dhead)


def pieces_of(values):
    first = lax.reduce_precision(values, 8, 7)
    second = lax.reduce_precision(values - first, 8, 7)
    return jnp.concatenate([first, second, values - first - second], axis=-1)


def lanes_of(*columns):
    filled = sum(c.shape[1] for c in columns)
    gap = jnp.zeros((columns[0].shape[0], LANES - filled), columns[0].dtype)
    return jnp.concatenate(columns + (gap,), axis=1)


def body(
    q_start, v_start, minv, geom_jac, pairs, gap_start, actions, act_map, batch_index,
    w_in, gain_one, w_up, w_down, gain_two, w_head, log_std, old_mu, advantage, returns,
):
    count = lax.axis_size(EVERY)
    chips = count // 2
    rows_up, ff = w_up.shape
    rows_down, width = w_down.shape
    obs = w_in.shape[0]
    heads = w_head.shape[1]
    acts = log_std.shape[0]
    per_peer = batch_index.shape[2]
    tokens = old_mu.shape[0]
    core = lax.axis_index("c").astype(jnp.int32).reshape(1)

    gains = jnp.stack([gain_one, gain_two])
    packed = pack(w_up, w_down, w_in, w_head, gains)
    beside = [packed]
    for step in (1, 3, 2):
        beside.append(lax.ppermute(packed, "x", [((i + step) % 4, i) for i in range(4)]))
    me = lax.axis_index("x")
    order = jnp.stack([beside[0], beside[1], beside[3], beside[2]])
    ordered = jnp.concatenate(
        [lax.dynamic_index_in_dim(order, (i - me) % 4, 0, keepdims=False) for i in range(4)],
        axis=1,
    )
    weights = lax.all_gather(ordered, ("z", "y", "c"), axis=0, tiled=True)

    picks = batch_index.reshape(1, count * per_peer)
    q_final, v_final, picked = rollout(
        q_start, v_start, minv, geom_jac, pairs, gap_start, actions, act_map, picks
    )
    row_width = picked.shape[1]
    arrived = lax.all_to_all(
        picked.reshape(count, per_peer, row_width), EVERY, split_axis=0, concat_axis=0, tiled=True
    )
    rows = arrived.reshape(tokens, row_width)
    aux = lanes_of(old_mu, advantage[:, None], returns[:, None])
    std = lanes_of(log_std[None])

    factor = loss_scale / (tokens * count)
    keep, send, pre, dsecond, norm_one, down, dhead, totals, gain_rows = forward(
        core, rows, aux, std, weights, ff, acts, factor
    )

    came = lax.ppermute(send, "c", SWAP)
    pair = (keep.astype(jnp.float32) + came.astype(jnp.float32)).astype(jnp.bfloat16)
    totals = totals[0, : acts + 1]
    totals = totals + lax.ppermute(totals, "c", SWAP)
    pair, dsecond = lax.optimization_barrier((pair, dsecond))
    down_came = lax.all_to_all(
        pair.reshape(chips, rows_down, width), WIRE, split_axis=0, concat_axis=0, tiled=True
    )
    grad_down = jnp.sum(down_came.astype(jnp.float32), axis=0)

    keep, send = backward(
        heads, core, rows, weights, gain_rows, pre, dsecond, norm_one, down, dhead
    )
    came = lax.ppermute(send, "c", SWAP)
    pair = (keep.astype(jnp.float32) + came.astype(jnp.float32)).reshape(chips, rows_up, -1)
    place = ff + LANES + heads + 2
    many = 3 * (acts + 1)
    line = jnp.zeros((pair.shape[2],), jnp.float32).at[place : place + many].set(pieces_of(totals))
    row_id = lax.broadcasted_iota(jnp.int32, pair.shape, 1)
    lane_id = lax.broadcasted_iota(jnp.int32, pair.shape, 2)
    special = (row_id == 0) & (lane_id >= place) & (lane_id < place + many)
    pair = jnp.where(special, line, pair).astype(jnp.bfloat16)
    up_came = lax.all_to_all(pair, WIRE, split_axis=0, concat_axis=0, tiled=True)
    summed = jnp.sum(up_came.astype(jnp.float32), axis=0)
    tail = summed[:, ff + LANES :]
    whole = summed[0, place : place + many].reshape(3, acts + 1).sum(axis=0)
    mean_loss = whole[acts] / (tokens * count)
    return (
        q_final,
        v_final,
        jnp.transpose(summed[:, ff : ff + obs]),
        tail[:, heads],
        summed[:, :ff],
        grad_down,
        tail[:, heads + 1],
        tail[:, :heads],
        whole[:acts],
        mean_loss,
    )


def solution(mesh):
    grid = Mesh(mesh.devices.reshape(4, 4, 4, 2), EVERY)
    placed = (
        P(None, EVERY),
        P(None, EVERY),
        P(None, None, EVERY),
        P(None, None, EVERY),
        P(None, None, EVERY),
        P(None, EVERY),
        P(None, None, EVERY),
        P(),
        P(EVERY, None, None),
        P(None, EVERY),
        P(EVERY),
        P(EVERY, None),
        P(EVERY, None),
        P(EVERY),
        P(EVERY, None),
        P(),
        P(EVERY, None),
        P(EVERY),
        P(EVERY),
    )
    return jax.shard_map(
        body,
        mesh=grid,
        in_specs=placed,
        out_specs=(
            P(None, EVERY),
            P(None, EVERY),
            P(None, EVERY),
            P(EVERY),
            P(EVERY, None),
            P(EVERY, None),
            P(EVERY),
            P(EVERY, None),
            P(),
            P(),
        ),
        check_vma=False,
    )
```

```python
import math

import jax
import jax.numpy as jnp
from jax import lax
from jax.experimental import pallas as pl
from jax.experimental.pallas import tpu as pltpu
from jax.sharding import Mesh
from jax.sharding import PartitionSpec as P

EVERY = ("x", "z", "y", "c")
WIRE = ("x", "z", "y")
LANES = 128
SWAP = [(0, 1), (1, 0)]
VMEM_LIMIT = 58 * 1024 * 1024

BINS = 32
ITERS = 8
time_step = 0.02
damping = 0.5
torque = 2.0
baumgarte = 0.2
soft_reg = 0.1
clip_eps = 0.2
value_coef = 0.5
entropy_coef = 0.01
loss_scale = 1024.0

VMEM = pl.BlockSpec(memory_space=pltpu.VMEM)
SMEM = pl.BlockSpec(memory_space=pltpu.SMEM)


def dot(a, b, dims, precision=None):
    return lax.dot_general(
        a, b, (dims, ((), ())), precision=precision, preferred_element_type=jnp.float32
    )


NN = ((1,), (0,))
NT = ((1,), (1,))
TN = ((0,), (0,))


def spread(row, rows):
    return jnp.broadcast_to(row, (rows, row.shape[-1]))


def rollout_kernel(
    q_ref, v_ref, minv_ref, geom_ref, pairs_ref, gap_ref, act_ref, map_ref, picks_ref,
    q_out, v_out, rows_out,
    select, jac, mob, dela, stored,
):
    geoms, dof, envs = geom_ref.shape
    cont = gap_ref.shape[0]
    steps, acts, _ = act_ref.shape

    @pl.loop(0, geoms)
    def _(g):
        first = (pairs_ref[0] == g).astype(jnp.float32)
        select[g] = first - (pairs_ref[1] == g).astype(jnp.float32)

    def by_rows(count, many, depth, left, right, out):
        @pl.loop(0, count // many)
        def _(block):
            sums = [jnp.zeros((cont, envs), jnp.float32) for _ in range(many)]
            for k in range(depth):
                held = right(k)
                for i in range(many):
                    sums[i] = sums[i] + spread(left(k, block * many + i), cont) * held
            for i in range(many):
                out[block * many + i] = sums[i]

    by_rows(dof, 3, geoms, lambda g, d: geom_ref[g, pl.ds(d, 1), :], lambda g: select[g], jac)
    by_rows(dof, 3, dof, lambda k, d: minv_ref[d, pl.ds(k, 1), :], lambda k: jac[k], mob)
    by_rows(cont, 4, dof, lambda d, e: mob[d, pl.ds(e, 1), :], lambda d: jac[d], dela)

    denom = jnp.full((cont, envs), soft_reg, jnp.float32)
    for e in range(cont):
        denom = denom + jnp.abs(dela[e])
    inverse = 1.0 / denom
    gap_rate = baumgarte / time_step
    q_first = q_ref[...]
    gap_first = gap_ref[...] * gap_rate

    def one_step(s, carry):
        q, v, lam = carry
        level = act_ref[s].astype(jnp.float32) * (2.0 / (BINS - 1)) - 1.0
        force = torque * dot(map_ref[...], level, NN, lax.Precision.HIGHEST) - damping * v
        pushed = jnp.zeros_like(v)
        for k in range(dof):
            pushed = pushed + minv_ref[k] * spread(force[k : k + 1], dof)
        vfree = v + time_step * pushed
        drift = vfree + gap_rate * (q - q_first)
        bias = gap_first
        for d in range(dof):
            bias = bias + jac[d] * spread(drift[d : d + 1], cont)

        def sweep(_, lam):
            push = [bias, jnp.zeros_like(bias)]
            for e in range(cont):
                push[e % 2] = push[e % 2] + dela[e] * spread(lam[e : e + 1], cont)
            return jnp.maximum(lam - (push[0] + push[1]) * inverse, 0.0)

        lam = lax.fori_loop(0, ITERS, sweep, lam)
        gained = [jnp.sum(mob[d] * lam, axis=0, keepdims=True) for d in range(dof)]
        v = vfree + jnp.concatenate(gained, axis=0)
        q = q + time_step * v
        stored[s] = jnp.concatenate([q, v, lam, level], axis=0).astype(jnp.bfloat16)
        return q, v, lam

    q, v, _ = lax.fori_loop(
        0, steps, one_step, (q_first, v_ref[...], jnp.zeros((cont, envs), jnp.float32))
    )
    q_out[...] = q
    v_out[...] = v

    picks = picks_ref.shape[1]
    block = 256
    for start in range(0, picks, block):
        wanted = picks_ref[:, start : start + block]
        found = jnp.zeros((stored.shape[1], block), jnp.float32)
        for s in range(steps):
            ids = lax.broadcasted_iota(jnp.int32, (envs, block), 0) + s * envs
            hit = (ids == wanted).astype(jnp.float32).astype(jnp.bfloat16)
            found = found + dot(stored[s], hit, NN)
        rows_out[start : start + block, :] = jnp.transpose(found).astype(jnp.bfloat16)


def rollout(q_start, v_start, minv, geom_jac, pairs, gap_start, actions, act_map, picks):
    geoms, dof, envs = geom_jac.shape
    cont = gap_start.shape[0]
    steps, acts, _ = actions.shape
    row = 2 * dof + cont + acts
    return pl.pallas_call(
        rollout_kernel,
        out_shape=(
            jax.ShapeDtypeStruct((dof, envs), jnp.float32),
            jax.ShapeDtypeStruct((dof, envs), jnp.float32),
            jax.ShapeDtypeStruct((picks.shape[1], row), jnp.bfloat16),
        ),
        in_specs=[VMEM] * 9,
        out_specs=(VMEM,) * 3,
        scratch_shapes=[
            pltpu.VMEM((geoms, cont, envs), jnp.float32),
            pltpu.VMEM((dof, cont, envs), jnp.float32),
            pltpu.VMEM((dof, cont, envs), jnp.float32),
            pltpu.VMEM((cont, cont, envs), jnp.float32),
            pltpu.VMEM((steps, row, envs), jnp.bfloat16),
        ],
        compiler_params=pltpu.CompilerParams(vmem_limit_bytes=VMEM_LIMIT),
        name="rollout",
    )(q_start, v_start, minv, geom_jac, pairs, gap_start, actions, act_map, picks)


TOKEN_BLOCK = 512
HBM = pl.BlockSpec(memory_space=pl.ANY)
GELU_RATE = math.sqrt(2.0 / math.pi)
GELU_CUBE = 0.044715 * GELU_RATE


def mean_square_root(values):
    return lax.rsqrt(jnp.mean(values * values, axis=1, keepdims=True) + 1e-05)


def norm_backward(grad, values, root):
    inner = jnp.mean(grad * values, axis=1, keepdims=True)
    return root * (grad - values * (root * root * inner))


def split_by_core(core, block, rows, keep_ref, send_ref, start, lane):
    count, columns = block.shape
    groups = block.reshape(count // (2 * rows), 2, rows, columns)
    half = count // 2
    at = pl.ds(pl.multiple_of(start, half), half)
    lanes = slice(lane, lane + columns)
    for which in range(2):
        part = groups[:, which].reshape(half, columns).astype(jnp.bfloat16)

        @pl.when(core == which)
        def _():
            keep_ref[at, lanes] = part

        @pl.when(core != which)
        def _():
            send_ref[at, lanes] = part


def pack_kernel(up_ref, down_ref, in_ref, head_ref, one_ref, two_ref, out_ref):
    rows, ff = up_ref.shape
    width = down_ref.shape[1]
    obs = in_ref.shape[1]
    heads = head_ref.shape[1]
    f32 = jnp.float32
    out_ref[:, :ff] = up_ref[...]
    down = down_ref[...].astype(f32)
    out_ref[:, ff : ff + width] = down[:rows].astype(jnp.bfloat16)
    out_ref[:, ff + width : ff + 2 * width] = down[rows:].astype(jnp.bfloat16)
    first = jnp.concatenate(
        [in_ref[...].astype(f32), jnp.zeros((rows, LANES - obs), f32)], axis=1
    )
    gains = jnp.concatenate(
        [one_ref[...].astype(f32), two_ref[...].astype(f32), jnp.zeros((LANES - 2, rows), f32)],
        axis=0,
    )
    second = pltpu.roll(jnp.transpose(gains), heads, 1)
    wide = jnp.concatenate(
        [head_ref[...].astype(f32), jnp.zeros((rows, LANES - heads), f32)], axis=1
    )
    both = jnp.concatenate([first, second + wide], axis=1)
    out_ref[:, ff + 2 * width :] = both.astype(jnp.bfloat16)


def pack(w_up, w_down, w_in, w_head, gain_one, gain_two):
    rows, ff = w_up.shape
    width = w_down.shape[1]
    return pl.pallas_call(
        pack_kernel,
        out_shape=jax.ShapeDtypeStruct((rows, ff + 2 * width + 2 * LANES), jnp.bfloat16),
        in_specs=[VMEM] * 6,
        out_specs=VMEM,
        name="pack",
    )(w_up, w_down, w_in, w_head, gain_one, gain_two)


def columns_in(weights_ref, parts, start, out_ref, sem):
    rows, total = weights_ref.shape
    columns = out_ref.shape[1]
    each = total // parts
    return [
        pltpu.make_async_copy(
            weights_ref.at[:, pl.ds(part * each + start, columns)],
            out_ref.at[pl.ds(part * rows, rows), :],
            sem.at[part],
        )
        for part in range(parts)
    ]


def forward_kernel(
    acts, factor, parts,
    core_ref, rows_ref, aux_ref, std_ref, weights_ref,
    keep_hbm, send_hbm, pre_hbm, dsecond_hbm, norm_hbm, down_hbm, dhead_ref, totals_ref, gains_ref,
    up_ref, both_ref, small_ref, down_ref, hidden_ref, pre_ref, dsecond_ref, norm_ref, keep_ref, send_ref,
    in_sem, out_sem,
):
    tokens = rows_ref.shape[0]
    width, ff = up_ref.shape
    load_small = columns_in(weights_ref, parts, ff + 2 * width, small_ref, in_sem.at[0])
    load_up = columns_in(weights_ref, parts, 0, up_ref, in_sem.at[1])
    load_both = columns_in(weights_ref, parts, ff, both_ref, in_sem.at[2])
    for copy in load_small + load_both + load_up:
        copy.start()

    inv_std = jnp.exp(-std_ref[...])
    lane = lax.broadcasted_iota(jnp.int32, (1, LANES), 1)
    is_act = lane < acts
    entropy = jnp.sum(jnp.where(is_act, std_ref[...], 0.0)) + 0.5 * acts * (
        1.0 + math.log(2.0 * math.pi)
    )
    dhead_ref[...] = jnp.zeros_like(dhead_ref)
    totals_ref[...] = jnp.zeros_like(totals_ref)
    low, high = 1.0 - clip_eps, 1.0 + clip_eps

    for copy in load_small:
        copy.wait()
    gains_ref[...] = jnp.transpose(small_ref[:, LANES:].astype(jnp.float32))[acts + 1 : acts + 9]
    gain_one = gains_ref[0:1, :]
    gain_two = gains_ref[1:2, :]

    many = 128
    for part, copy in enumerate(load_both):
        copy.wait()

        @pl.loop(part * (width // parts) // many, (part + 1) * (width // parts) // many)
        def _(block):
            at = pl.ds(pl.multiple_of(block * many, many), many)
            halves = both_ref[at, :].astype(jnp.float32).reshape(many // 8, 8, 2 * width)
            mixed = jnp.stack([halves[:, :, :width], halves[:, :, width:]], axis=1)
            to = pl.ds(pl.multiple_of(block * 2 * many, 2 * many), 2 * many)
            down_ref[to, :] = mixed.reshape(2 * many, width).astype(jnp.bfloat16)

    down_out = pltpu.make_async_copy(down_ref, down_hbm, out_sem.at[0])
    down_out.start()
    for copy in load_up:
        copy.wait()

    @pl.loop(0, tokens // TOKEN_BLOCK)
    def _(block):
        at = pl.ds(pl.multiple_of(block * TOKEN_BLOCK, TOKEN_BLOCK), TOKEN_BLOCK)
        rows = rows_ref[at, :]
        first = dot(rows, small_ref[:, :LANES], NT)
        norm_one = (first * mean_square_root(first) * gain_one).astype(jnp.bfloat16)
        norm_ref[at, :] = norm_one
        second = first
        chunk = 512
        for start in range(0, ff, chunk):
            lanes = slice(start, start + chunk)
            pre = dot(norm_one, up_ref[:, lanes], NN)
            pre_ref[at, lanes] = pre.astype(jnp.bfloat16)
            bent = jnp.tanh(pre * (GELU_RATE + GELU_CUBE * (pre * pre)))
            half = 0.5 * pre
            hidden = (half + half * bent).astype(jnp.bfloat16)
            hidden_ref[at, lanes] = hidden
            second = second + dot(hidden, down_ref[lanes, :], NN)
        pltpu.make_async_copy(pre_ref.at[at, :], pre_hbm.at[at, :], out_sem.at[1]).start()
        pltpu.make_async_copy(norm_ref.at[at, :], norm_hbm.at[at, :], out_sem.at[2]).start()
        root_two = mean_square_root(second)
        scaled = second * root_two
        norm_two = (scaled * gain_two).astype(jnp.bfloat16)
        head = dot(norm_two, small_ref[:, LANES:], NN)

        aux = aux_ref[at, :]
        advantage = aux[:, acts : acts + 1]
        returns = aux[:, acts + 1 : acts + 2]
        taken = pltpu.roll(rows.astype(jnp.float32), acts, 1)
        from_old = jnp.where(is_act, (taken - aux) * inv_std, 0.0)
        from_new = jnp.where(is_act, (taken - head) * inv_std, 0.0)
        apart = from_old * from_old - from_new * from_new
        ratio = jnp.exp(0.5 * jnp.sum(apart, axis=1, keepdims=True))
        free = ratio * advantage
        held = jnp.clip(ratio, low, high) * advantage
        missed = head[:, acts : acts + 1] - returns
        losses = (
            -jnp.minimum(free, held)
            + (0.5 * value_coef) * missed * missed
            - entropy_coef * entropy
        )
        on_free = jnp.where(free < held, 1.0, jnp.where(free == held, 0.5, 0.0))
        inside = jnp.where(
            (ratio > low) & (ratio < high),
            1.0,
            jnp.where((ratio == low) | (ratio == high), 0.5, 0.0),
        )
        dratio = -advantage * (on_free + (1.0 - on_free) * inside)
        dlog = (factor * dratio) * ratio
        dhead = jnp.where(
            is_act,
            dlog * (from_new * inv_std),
            jnp.where(lane == acts, (factor * value_coef) * missed, 0.0),
        )
        dstd = jnp.where(is_act, -dlog * apart - factor * entropy_coef, 0.0)
        both = jnp.where(lane == acts, losses, dstd)
        totals_ref[...] += jnp.sum(both, axis=0, keepdims=True)

        dhead = dhead.astype(jnp.bfloat16)
        dnorm = dot(dhead, small_ref[:, LANES:], NT)
        dhead_ref[0:LANES, :] += dot(dhead, norm_two, TN)
        dhead_ref[LANES : LANES + 1, :] += jnp.sum(dnorm * scaled, axis=0, keepdims=True)
        dsecond = norm_backward(dnorm * gain_two, second, root_two)
        dsecond_ref[at, :] = dsecond.astype(jnp.bfloat16)
        pltpu.make_async_copy(dsecond_ref.at[at, :], dsecond_hbm.at[at, :], out_sem.at[3]).start()

    chunk = 256

    @pl.loop(0, ff // chunk)
    def _(block):
        lanes = pl.ds(pl.multiple_of(block * chunk, chunk), chunk)
        grad = dot(hidden_ref[:, lanes], dsecond_ref[...], TN)
        start = block * (chunk // 2)
        split_by_core(core_ref[0], grad, 16, keep_ref, send_ref, start, 0)
        at = pl.ds(pl.multiple_of(start, chunk // 2), chunk // 2)
        pltpu.make_async_copy(keep_ref.at[at, :], keep_hbm.at[at, :], out_sem.at[4]).start()
        pltpu.make_async_copy(send_ref.at[at, :], send_hbm.at[at, :], out_sem.at[5]).start()

    down_out.wait()
    outs = ((pre_ref, pre_hbm), (norm_ref, norm_hbm), (dsecond_ref, dsecond_hbm))
    for place, (here, there) in enumerate(outs + ((keep_ref, keep_hbm), (send_ref, send_hbm))):
        pltpu.make_async_copy(here, there, out_sem.at[place + 1]).wait()


def forward(core, rows, aux, std, weights, ff, acts, factor):
    tokens = rows.shape[0]
    group, total = weights.shape
    width = 1024
    parts = width // group
    bf16, f32 = jnp.bfloat16, jnp.float32
    shapes = [(ff // 2, width), (ff // 2, width), (tokens, ff), (tokens, width), (tokens, width), (ff, width)]
    return pl.pallas_call(
        lambda *refs: forward_kernel(acts, factor, parts, *refs),
        out_shape=tuple(jax.ShapeDtypeStruct(shape, bf16) for shape in shapes)
        + (
            jax.ShapeDtypeStruct((LANES + 8, width), f32),
            jax.ShapeDtypeStruct((1, LANES), f32),
            jax.ShapeDtypeStruct((8, width), f32),
        ),
        in_specs=[SMEM] + [VMEM] * 3 + [HBM],
        out_specs=(HBM,) * 6 + (VMEM,) * 3,
        scratch_shapes=[
            pltpu.VMEM((width, ff), bf16),
            pltpu.VMEM((width, 2 * width), bf16),
            pltpu.VMEM((width, 2 * LANES), bf16),
            pltpu.VMEM((ff, width), bf16),
            pltpu.VMEM((tokens, ff), bf16),
            pltpu.VMEM((tokens, ff), bf16),
            pltpu.VMEM((tokens, width), bf16),
            pltpu.VMEM((tokens, width), bf16),
            pltpu.VMEM((ff // 2, width), bf16),
            pltpu.VMEM((ff // 2, width), bf16),
            pltpu.SemaphoreType.DMA((3, parts)),
            pltpu.SemaphoreType.DMA((6,)),
        ],
        compiler_params=pltpu.CompilerParams(vmem_limit_bytes=VMEM_LIMIT),
        cost_estimate=pl.CostEstimate(
            flops=6 * tokens * width * ff, bytes_accessed=30 << 20, transcendentals=tokens * ff
        ),
        name="forward",
    )(core, rows, aux, std, weights)


def backward_kernel(
    heads, parts,
    core_ref, rows_ref, weights_ref, gains_ref, pre_hbm, dsecond_hbm, norm_hbm, down_hbm, dhead_ref,
    keep_hbm, send_hbm,
    up_ref, win_ref, down_ref, pre_ref, dsecond_ref, norm_ref, dpre_ref, din_ref, dgain_ref, keep_ref, send_ref,
    in_sem, out_sem,
):
    tokens = rows_ref.shape[0]
    width, ff = up_ref.shape
    load_win = columns_in(weights_ref, parts, ff + 2 * width, win_ref, in_sem.at[0])
    load_up = columns_in(weights_ref, parts, 0, up_ref, in_sem.at[1])
    pairs = ((dsecond_hbm, dsecond_ref), (down_hbm, down_ref), (pre_hbm, pre_ref), (norm_hbm, norm_ref))
    loads = [
        pltpu.make_async_copy(there, here, in_sem.at[2, place])
        for place, (there, here) in enumerate(pairs)
    ]
    for copy in load_win + loads[:3] + load_up + loads[3:]:
        copy.start()
    gain_one = gains_ref[0:1, :]
    din_ref[...] = jnp.zeros_like(din_ref)
    dgain_ref[...] = jnp.zeros_like(dgain_ref)
    for copy in load_win + loads[:3] + load_up:
        copy.wait()

    @pl.loop(0, tokens // TOKEN_BLOCK)
    def _(block):
        at = pl.ds(pl.multiple_of(block * TOKEN_BLOCK, TOKEN_BLOCK), TOKEN_BLOCK)
        rows = rows_ref[at, :]
        first = dot(rows, win_ref[...], NT)
        root = mean_square_root(first)
        dsecond = dsecond_ref[at, :]
        dnorm = jnp.zeros((TOKEN_BLOCK, width), jnp.float32)
        chunk = 512
        for start in range(0, ff, chunk):
            lanes = slice(start, start + chunk)
            dhidden = dot(dsecond, down_ref[lanes, :], NT)
            pre = pre_ref[at, lanes].astype(jnp.float32)
            square = pre * pre
            bent = jnp.tanh(pre * (GELU_RATE + GELU_CUBE * square))
            half = 0.5 * pre
            slope = 0.5 + 0.5 * bent + (half - half * (bent * bent)) * (
                GELU_RATE + (3.0 * GELU_CUBE) * square
            )
            dpre = (dhidden * slope).astype(jnp.bfloat16)
            dpre_ref[at, lanes] = dpre
            dnorm = dnorm + dot(dpre, up_ref[:, lanes], NT)
        dgain_ref[0:1, :] += jnp.sum(dnorm * (first * root), axis=0, keepdims=True)
        dfirst = dsecond.astype(jnp.float32) + norm_backward(dnorm * gain_one, first, root)
        din_ref[...] += dot(rows, dfirst.astype(jnp.bfloat16), TN)

    loads[3].wait()
    chunk = 256
    ids = lax.broadcasted_iota(jnp.int32, (LANES, chunk), 0)

    @pl.loop(0, width // chunk)
    def _(block):
        lanes = pl.ds(pl.multiple_of(block * chunk, chunk), chunk)
        core = core_ref[0]
        half = block * (chunk // 2)
        for start in range(0, ff, 1024):
            grad = dot(norm_ref[:, lanes], dpre_ref[:, start : start + 1024], TN)
            split_by_core(core, grad, 8, keep_ref, send_ref, half, start)
        split_by_core(core, jnp.transpose(din_ref[:, lanes]), 8, keep_ref, send_ref, half, ff)
        tail = jnp.where(ids == heads, dgain_ref[0:1, lanes], dhead_ref[0:LANES, lanes])
        tail = jnp.where(ids == heads + 1, dhead_ref[LANES : LANES + 1, lanes], tail)
        split_by_core(core, jnp.transpose(tail), 8, keep_ref, send_ref, half, ff + LANES)
        at = pl.ds(pl.multiple_of(half, chunk // 2), chunk // 2)
        pltpu.make_async_copy(keep_ref.at[at, :], keep_hbm.at[at, :], out_sem.at[0]).start()
        pltpu.make_async_copy(send_ref.at[at, :], send_hbm.at[at, :], out_sem.at[1]).start()

    pltpu.make_async_copy(keep_ref, keep_hbm, out_sem.at[0]).wait()
    pltpu.make_async_copy(send_ref, send_hbm, out_sem.at[1]).wait()


def backward(heads, core, rows, weights, gains, pre, dsecond, norm_one, down, dhead):
    tokens, ff = pre.shape
    width = dsecond.shape[1]
    parts = width // weights.shape[0]
    bf16, f32 = jnp.bfloat16, jnp.float32
    out = jax.ShapeDtypeStruct((width // 2, ff + 2 * LANES), bf16)
    return pl.pallas_call(
        lambda *refs: backward_kernel(heads, parts, *refs),
        out_shape=(out, out),
        in_specs=[SMEM, VMEM, HBM, VMEM] + [HBM] * 4 + [VMEM],
        out_specs=(HBM, HBM),
        scratch_shapes=[
            pltpu.VMEM((width, ff), bf16),
            pltpu.VMEM((width, LANES), bf16),
            pltpu.VMEM((ff, width), bf16),
            pltpu.VMEM((tokens, ff), bf16),
            pltpu.VMEM((tokens, width), bf16),
            pltpu.VMEM((tokens, width), bf16),
            pltpu.VMEM((tokens, ff), bf16),
            pltpu.VMEM((LANES, width), f32),
            pltpu.VMEM((8, width), f32),
            pltpu.VMEM(out.shape, bf16),
            pltpu.VMEM(out.shape, bf16),
            pltpu.SemaphoreType.DMA((3, max(parts, 4))),
            pltpu.SemaphoreType.DMA((2,)),
        ],
        compiler_params=pltpu.CompilerParams(vmem_limit_bytes=VMEM_LIMIT),
        cost_estimate=pl.CostEstimate(
            flops=6 * tokens * width * ff, bytes_accessed=30 << 20, transcendentals=tokens * ff
        ),
        name="backward",
    )(core, rows, weights, gains, pre, dsecond, norm_one, down, dhead)


def pair_kernel(keep_ref, came_ref, out_ref):
    total = keep_ref[...].astype(jnp.float32) + came_ref[...].astype(jnp.float32)
    out_ref[...] = total.astype(jnp.bfloat16)


def pair_totals_kernel(place, count, rows, mine_ref, other_ref, keep_ref, came_ref, out_ref):
    f32, bf16 = jnp.float32, jnp.bfloat16
    cut = keep_ref.shape[1] - LANES
    pair_kernel(keep_ref.at[:, :cut], came_ref.at[:, :cut], out_ref.at[:, :cut])
    lane = lax.broadcasted_iota(jnp.int32, (8, LANES), 1)
    totals = jnp.broadcast_to(mine_ref[...] + other_ref[...], (8, LANES))
    totals = jnp.where(lane < count, totals, 0.0)
    first = totals.astype(bf16).astype(f32)
    second = (totals - first).astype(bf16).astype(f32)
    third = totals - first - second
    line = (
        pltpu.roll(first, place, 1)
        + pltpu.roll(second, place + count, 1)
        + pltpu.roll(third, place + 2 * count, 1)
    )
    tail = keep_ref[:, cut:].astype(f32) + came_ref[:, cut:].astype(f32)
    row = lax.broadcasted_iota(jnp.int32, tail.shape, 0) % rows
    lane = lax.broadcasted_iota(jnp.int32, tail.shape, 1)
    special = (row == 0) & (lane >= place) & (lane < place + 3 * count)
    out_ref[:, cut:] = jnp.where(special, line[0:1], tail).astype(bf16)


def pair_sum(keep, came, kernel=pair_kernel, small=()):
    rows, columns = keep.shape
    block = pl.BlockSpec((rows // 4, columns), lambda i: (i, 0))
    whole = pl.BlockSpec((1, LANES), lambda i: (0, 0))
    return pl.pallas_call(
        kernel,
        out_shape=jax.ShapeDtypeStruct(keep.shape, keep.dtype),
        grid=(4,),
        in_specs=[whole] * len(small) + [block, block],
        out_specs=block,
        compiler_params=pltpu.CompilerParams(vmem_limit_bytes=VMEM_LIMIT),
        name="pair",
    )(*small, keep, came)


def finish_kernel(
    acts, came_ref, in_ref, one_ref, up_ref, two_ref, head_ref, std_ref, loss_ref
):
    ff = up_ref.shape[1]
    obs = in_ref.shape[1]
    heads = head_ref.shape[1]
    total = came_ref[0].astype(jnp.float32)
    for chip in range(1, came_ref.shape[0]):
        total = total + came_ref[chip].astype(jnp.float32)
    up_ref[...] = total[:, :ff]
    in_ref[...] = total[:, ff : ff + obs]
    tail = total[:, ff + LANES :]
    head_ref[...] = tail[:, :heads]
    flipped = jnp.transpose(tail)
    one_ref[...] = flipped[heads : heads + 1]
    two_ref[...] = flipped[heads + 1 : heads + 2]
    count = acts + 1
    place = heads + 2
    whole = (
        pltpu.roll(tail, LANES - place, 1)
        + pltpu.roll(tail, LANES - place - count, 1)
        + pltpu.roll(tail, LANES - place - 2 * count, 1)
    )[0:1]
    std_ref[...] = whole[:, :acts]
    loss_ref[...] = whole[:, acts : acts + 1]


def finish(came, ff, obs, heads, acts):
    rows = came.shape[1]
    shapes = ((rows, obs), (1, rows), (rows, ff), (1, rows), (rows, heads), (1, acts), (1, 1))
    return pl.pallas_call(
        lambda *refs: finish_kernel(acts, *refs),
        out_shape=tuple(jax.ShapeDtypeStruct(shape, jnp.float32) for shape in shapes),
        in_specs=[VMEM],
        out_specs=(VMEM,) * 7,
        compiler_params=pltpu.CompilerParams(vmem_limit_bytes=VMEM_LIMIT),
        name="finish",
    )(came)


def lanes_of(*columns):
    filled = sum(c.shape[1] for c in columns)
    gap = jnp.zeros((columns[0].shape[0], LANES - filled), columns[0].dtype)
    return jnp.concatenate(columns + (gap,), axis=1)


def body(
    q_start, v_start, minv, geom_jac, pairs, gap_start, actions, act_map, batch_index,
    w_in, gain_one, w_up, w_down, gain_two, w_head, log_std, old_mu, advantage, returns,
):
    count = lax.axis_size(EVERY)
    chips = count // 2
    rows_up, ff = w_up.shape
    rows_down, width = w_down.shape
    obs = w_in.shape[0]
    heads = w_head.shape[1]
    acts = log_std.shape[0]
    per_peer = batch_index.shape[2]
    tokens = old_mu.shape[0]
    core = lax.axis_index("c").astype(jnp.int32).reshape(1)

    packed = pack(
        w_up, w_down, jnp.transpose(w_in), w_head, gain_one.reshape(1, -1), gain_two.reshape(1, -1)
    )
    beside = [packed]
    for step in (1, 3, 2):
        beside.append(lax.ppermute(packed, "x", [((i + step) % 4, i) for i in range(4)]))
    me = lax.axis_index("x")
    order = jnp.stack([beside[0], beside[1], beside[3], beside[2]])
    ordered = jnp.concatenate(
        [lax.dynamic_index_in_dim(order, (i - me) % 4, 0, keepdims=False) for i in range(4)],
        axis=1,
    )
    weights = lax.all_gather(ordered, ("z", "y", "c"), axis=0, tiled=True)

    picks = batch_index.reshape(1, count * per_peer)
    q_final, v_final, picked = rollout(
        q_start, v_start, minv, geom_jac, pairs, gap_start, actions, act_map, picks
    )
    row_width = picked.shape[1]
    arrived = lax.all_to_all(
        picked.reshape(count, per_peer, row_width), EVERY, split_axis=0, concat_axis=0, tiled=True
    )
    rows = arrived.reshape(tokens, row_width)
    aux = lanes_of(old_mu, advantage[:, None], returns[:, None])
    std = lanes_of(log_std[None])

    factor = loss_scale / (tokens * count)
    keep, send, pre, dsecond, norm_one, down, dhead, totals, gain_rows = forward(
        core, rows, aux, std, weights, ff, acts, factor
    )

    pair = pair_sum(keep, lax.ppermute(send, "c", SWAP))
    pair, dsecond = lax.optimization_barrier((pair, dsecond))
    down_came = lax.all_to_all(
        pair.reshape(chips, rows_down, width), WIRE, split_axis=0, concat_axis=0, tiled=True
    )
    other_totals = lax.ppermute(totals, "c", SWAP)
    keep, send = backward(
        heads, core, rows, weights, gain_rows, pre, dsecond, norm_one, down, dhead
    )
    send, down_came = lax.optimization_barrier((send, down_came))
    grad_down = jnp.sum(down_came.astype(jnp.float32), axis=0)

    pair = pair_sum(
        keep,
        lax.ppermute(send, "c", SWAP),
        lambda *refs: pair_totals_kernel(heads + 2, acts + 1, rows_up, *refs),
        (totals, other_totals),
    )
    up_came = lax.all_to_all(
        pair.reshape(chips, rows_up, -1), WIRE, split_axis=0, concat_axis=0, tiled=True
    )
    grad_in, grad_one, grad_up, grad_two, grad_head, grad_std, loss = finish(
        up_came, ff, obs, heads, acts
    )
    return (
        q_final,
        v_final,
        jnp.transpose(grad_in),
        grad_one.reshape(-1),
        grad_up,
        grad_down,
        grad_two.reshape(-1),
        grad_head,
        grad_std.reshape(-1),
        loss.reshape(()) / (tokens * count),
    )


def solution(mesh):
    grid = Mesh(mesh.devices.reshape(4, 4, 4, 2), EVERY)
    placed = (
        P(None, EVERY),
        P(None, EVERY),
        P(None, None, EVERY),
        P(None, None, EVERY),
        P(None, None, EVERY),
        P(None, EVERY),
        P(None, None, EVERY),
        P(),
        P(EVERY, None, None),
        P(None, EVERY),
        P(EVERY),
        P(EVERY, None),
        P(EVERY, None),
        P(EVERY),
        P(EVERY, None),
        P(),
        P(EVERY, None),
        P(EVERY),
        P(EVERY),
    )
    return jax.shard_map(
        body,
        mesh=grid,
        in_specs=placed,
        out_specs=(
            P(None, EVERY),
            P(None, EVERY),
            P(None, EVERY),
            P(EVERY),
            P(EVERY, None),
            P(EVERY, None),
            P(EVERY),
            P(EVERY, None),
            P(),
            P(),
        ),
        check_vma=False,
    )
```

```python
import math

import jax
import jax.numpy as jnp
from jax import lax
from jax.experimental import pallas as pl
from jax.experimental.pallas import tpu as pltpu
from jax.sharding import Mesh
from jax.sharding import PartitionSpec as P

EVERY = ("x", "z", "y", "c")
WIRE = ("x", "z", "y")
LANES = 128
SWAP = [(0, 1), (1, 0)]
VMEM_LIMIT = 46 * 1024 * 1024

BINS = 32
ITERS = 8
time_step = 0.02
damping = 0.5
torque = 2.0
baumgarte = 0.2
soft_reg = 0.1
clip_eps = 0.2
value_coef = 0.5
entropy_coef = 0.01
loss_scale = 1024.0

VMEM = pl.BlockSpec(memory_space=pltpu.VMEM)
SMEM = pl.BlockSpec(memory_space=pltpu.SMEM)


def dot(a, b, dims, precision=None):
    return lax.dot_general(
        a, b, (dims, ((), ())), precision=precision, preferred_element_type=jnp.float32
    )


NN = ((1,), (0,))
NT = ((1,), (1,))
TN = ((0,), (0,))


def spread(row, rows):
    return jnp.broadcast_to(row, (rows, row.shape[-1]))


def rollout_kernel(
    q_ref, v_ref, minv_ref, geom_ref, pairs_ref, gap_ref, act_ref, map_ref, picks_ref,
    q_out, v_out, rows_out,
    select, jac, mob, dela, stored,
):
    geoms, dof, envs = geom_ref.shape
    cont = gap_ref.shape[0]
    steps, acts, _ = act_ref.shape

    @pl.loop(0, geoms)
    def _(g):
        first = (pairs_ref[0] == g).astype(jnp.float32)
        select[g] = first - (pairs_ref[1] == g).astype(jnp.float32)

    def by_rows(count, many, depth, left, right, out):
        @pl.loop(0, count // many)
        def _(block):
            sums = [jnp.zeros((cont, envs), jnp.float32) for _ in range(many)]
            for k in range(depth):
                held = right(k)
                for i in range(many):
                    sums[i] = sums[i] + spread(left(k, block * many + i), cont) * held
            for i in range(many):
                out[block * many + i] = sums[i]

    by_rows(dof, 3, geoms, lambda g, d: geom_ref[g, pl.ds(d, 1), :], lambda g: select[g], jac)
    by_rows(dof, 3, dof, lambda k, d: minv_ref[d, pl.ds(k, 1), :], lambda k: jac[k], mob)
    by_rows(cont, 4, dof, lambda d, e: mob[d, pl.ds(e, 1), :], lambda d: jac[d], dela)

    denom = jnp.full((cont, envs), soft_reg, jnp.float32)
    for e in range(cont):
        denom = denom + jnp.abs(dela[e])
    inverse = 1.0 / denom
    gap_rate = baumgarte / time_step
    q_first = q_ref[...]
    gap_first = gap_ref[...] * gap_rate

    def one_step(s, carry):
        q, v, lam = carry
        level = act_ref[s].astype(jnp.float32) * (2.0 / (BINS - 1)) - 1.0
        force = torque * dot(map_ref[...], level, NN, lax.Precision.HIGHEST) - damping * v
        pushed = jnp.zeros_like(v)
        for k in range(dof):
            pushed = pushed + minv_ref[k] * spread(force[k : k + 1], dof)
        vfree = v + time_step * pushed
        drift = vfree + gap_rate * (q - q_first)
        bias = gap_first
        for d in range(dof):
            bias = bias + jac[d] * spread(drift[d : d + 1], cont)

        def sweep(_, lam):
            push = [bias, jnp.zeros_like(bias)]
            for e in range(cont):
                push[e % 2] = push[e % 2] + dela[e] * spread(lam[e : e + 1], cont)
            return jnp.maximum(lam - (push[0] + push[1]) * inverse, 0.0)

        lam = lax.fori_loop(0, ITERS, sweep, lam)
        gained = [jnp.sum(mob[d] * lam, axis=0, keepdims=True) for d in range(dof)]
        v = vfree + jnp.concatenate(gained, axis=0)
        q = q + time_step * v
        stored[s] = jnp.concatenate([q, v, lam, level], axis=0).astype(jnp.bfloat16)
        return q, v, lam

    q, v, _ = lax.fori_loop(
        0, steps, one_step, (q_first, v_ref[...], jnp.zeros((cont, envs), jnp.float32))
    )
    q_out[...] = q
    v_out[...] = v

    picks = picks_ref.shape[1]
    block = 256
    for start in range(0, picks, block):
        wanted = picks_ref[:, start : start + block]
        found = jnp.zeros((stored.shape[1], block), jnp.float32)
        for s in range(steps):
            ids = lax.broadcasted_iota(jnp.int32, (envs, block), 0) + s * envs
            hit = (ids == wanted).astype(jnp.float32).astype(jnp.bfloat16)
            found = found + dot(stored[s], hit, NN)
        rows_out[start : start + block, :] = jnp.transpose(found).astype(jnp.bfloat16)


def rollout(q_start, v_start, minv, geom_jac, pairs, gap_start, actions, act_map, picks):
    geoms, dof, envs = geom_jac.shape
    cont = gap_start.shape[0]
    steps, acts, _ = actions.shape
    row = 2 * dof + cont + acts
    return pl.pallas_call(
        rollout_kernel,
        out_shape=(
            jax.ShapeDtypeStruct((dof, envs), jnp.float32),
            jax.ShapeDtypeStruct((dof, envs), jnp.float32),
            jax.ShapeDtypeStruct((picks.shape[1], row), jnp.bfloat16),
        ),
        in_specs=[VMEM] * 9,
        out_specs=(VMEM,) * 3,
        scratch_shapes=[
            pltpu.VMEM((geoms, cont, envs), jnp.float32),
            pltpu.VMEM((dof, cont, envs), jnp.float32),
            pltpu.VMEM((dof, cont, envs), jnp.float32),
            pltpu.VMEM((cont, cont, envs), jnp.float32),
            pltpu.VMEM((steps, row, envs), jnp.bfloat16),
        ],
        compiler_params=pltpu.CompilerParams(vmem_limit_bytes=VMEM_LIMIT),
        name="rollout",
    )(q_start, v_start, minv, geom_jac, pairs, gap_start, actions, act_map, picks)


TOKEN_BLOCK = 512
HBM = pl.BlockSpec(memory_space=pl.ANY)
GELU_RATE = math.sqrt(2.0 / math.pi)
GELU_CUBE = 0.044715 * GELU_RATE


def mean_square_root(values):
    return lax.rsqrt(jnp.mean(values * values, axis=1, keepdims=True) + 1e-05)


def norm_backward(grad, values, root):
    inner = jnp.mean(grad * values, axis=1, keepdims=True)
    return root * (grad - values * (root * root * inner))


def split_by_core(core, block, rows, keep_ref, send_ref, start, lane):
    count, columns = block.shape
    groups = block.reshape(count // (2 * rows), 2, rows, columns)
    half = count // 2
    at = pl.ds(pl.multiple_of(start, half), half)
    lanes = slice(lane, lane + columns)
    for which in range(2):
        part = groups[:, which].reshape(half, columns).astype(jnp.bfloat16)

        @pl.when(core == which)
        def _():
            keep_ref[at, lanes] = part

        @pl.when(core != which)
        def _():
            send_ref[at, lanes] = part


def pack_kernel(up_ref, down_ref, in_ref, head_ref, one_ref, two_ref, out_ref):
    rows, ff = up_ref.shape
    width = down_ref.shape[1]
    obs = in_ref.shape[1]
    heads = head_ref.shape[1]
    f32 = jnp.float32
    out_ref[:, :ff] = up_ref[...]
    down = down_ref[...].astype(f32)
    out_ref[:, ff : ff + width] = down[:rows].astype(jnp.bfloat16)
    out_ref[:, ff + width : ff + 2 * width] = down[rows:].astype(jnp.bfloat16)
    first = jnp.concatenate(
        [in_ref[...].astype(f32), jnp.zeros((rows, LANES - obs), f32)], axis=1
    )
    gains = jnp.concatenate(
        [one_ref[...].astype(f32), two_ref[...].astype(f32), jnp.zeros((LANES - 2, rows), f32)],
        axis=0,
    )
    second = pltpu.roll(jnp.transpose(gains), heads, 1)
    wide = jnp.concatenate(
        [head_ref[...].astype(f32), jnp.zeros((rows, LANES - heads), f32)], axis=1
    )
    both = jnp.concatenate([first, second + wide], axis=1)
    out_ref[:, ff + 2 * width :] = both.astype(jnp.bfloat16)


def pack(w_up, w_down, w_in, w_head, gain_one, gain_two):
    rows, ff = w_up.shape
    width = w_down.shape[1]
    return pl.pallas_call(
        pack_kernel,
        out_shape=jax.ShapeDtypeStruct((rows, ff + 2 * width + 2 * LANES), jnp.bfloat16),
        in_specs=[VMEM] * 6,
        out_specs=VMEM,
        name="pack",
    )(w_up, w_down, w_in, w_head, gain_one, gain_two)


def columns_in(weights_ref, parts, first, start, out_ref, sem):
    rows, total = weights_ref.shape
    columns = out_ref.shape[1]
    each = total // parts
    return [
        pltpu.make_async_copy(
            weights_ref.at[:, pl.ds(part * each + start, columns)],
            out_ref.at[pl.ds(pl.multiple_of((first + part) % parts * rows, rows), rows), :],
            sem.at[part],
        )
        for part in range(parts)
    ]


def forward_kernel(
    acts, factor, parts,
    place_ref, rows_ref, aux_ref, std_ref, weights_ref,
    keep_ref, send_hbm, pre_hbm, dsecond_hbm, norm_hbm, down_hbm, dhead_ref, totals_ref, gains_ref,
    up_ref, both_ref, small_ref, down_ref, hidden_ref, pre_ref, dsecond_ref, norm_ref, send_ref,
    in_sem, out_sem,
):
    tokens = rows_ref.shape[0]
    width, ff = up_ref.shape
    load_small = columns_in(weights_ref, parts, place_ref[1], ff + 2 * width, small_ref, in_sem.at[0])
    load_up = columns_in(weights_ref, parts, place_ref[1], 0, up_ref, in_sem.at[1])
    load_both = columns_in(weights_ref, parts, place_ref[1], ff, both_ref, in_sem.at[2])
    for copy in load_small + load_both + load_up:
        copy.start()

    inv_std = jnp.exp(-std_ref[...])
    lane = lax.broadcasted_iota(jnp.int32, (1, LANES), 1)
    is_act = lane < acts
    entropy = jnp.sum(jnp.where(is_act, std_ref[...], 0.0)) + 0.5 * acts * (
        1.0 + math.log(2.0 * math.pi)
    )
    dhead_ref[...] = jnp.zeros_like(dhead_ref)
    totals_ref[...] = jnp.zeros_like(totals_ref)
    low, high = 1.0 - clip_eps, 1.0 + clip_eps

    for copy in load_small:
        copy.wait()
    gains_ref[...] = jnp.transpose(small_ref[:, LANES:].astype(jnp.float32))[acts + 1 : acts + 9]
    gain_one = gains_ref[0:1, :]
    gain_two = gains_ref[1:2, :]

    many = 128
    for part, copy in enumerate(load_both):
        copy.wait()

        @pl.loop(0, width // parts // many)
        def _(step):
            block = (place_ref[1] + part) % parts * (width // parts // many) + step
            at = pl.ds(pl.multiple_of(block * many, many), many)
            halves = both_ref[at, :].astype(jnp.float32).reshape(many // 8, 8, 2 * width)
            mixed = jnp.stack([halves[:, :, :width], halves[:, :, width:]], axis=1)
            to = pl.ds(pl.multiple_of(block * 2 * many, 2 * many), 2 * many)
            down_ref[to, :] = mixed.reshape(2 * many, width).astype(jnp.bfloat16)

    down_out = pltpu.make_async_copy(down_ref, down_hbm, out_sem.at[0])
    down_out.start()
    for copy in load_up:
        copy.wait()

    @pl.loop(0, tokens // TOKEN_BLOCK)
    def _(block):
        at = pl.ds(pl.multiple_of(block * TOKEN_BLOCK, TOKEN_BLOCK), TOKEN_BLOCK)
        rows = rows_ref[at, :]
        first = dot(rows, small_ref[:, :LANES], NT)
        norm_one = (first * mean_square_root(first) * gain_one).astype(jnp.bfloat16)
        norm_ref[at, :] = norm_one
        second = first
        chunk = 1024
        for start in range(0, ff, chunk):
            lanes = slice(start, start + chunk)
            pre = dot(norm_one, up_ref[:, lanes], NN)
            pre_ref[at, lanes] = pre.astype(jnp.bfloat16)
            bent = jnp.tanh(pre * (GELU_RATE + GELU_CUBE * (pre * pre)))
            half = 0.5 * pre
            hidden = (half + half * bent).astype(jnp.bfloat16)
            hidden_ref[at, lanes] = hidden
            second = second + dot(hidden, down_ref[lanes, :], NN)
        pltpu.make_async_copy(pre_ref.at[at, :], pre_hbm.at[at, :], out_sem.at[1]).start()
        pltpu.make_async_copy(norm_ref.at[at, :], norm_hbm.at[at, :], out_sem.at[2]).start()
        root_two = mean_square_root(second)
        scaled = second * root_two
        norm_two = (scaled * gain_two).astype(jnp.bfloat16)
        head = dot(norm_two, small_ref[:, LANES:], NN)

        aux = aux_ref[at, :]
        advantage = aux[:, acts : acts + 1]
        returns = aux[:, acts + 1 : acts + 2]
        taken = pltpu.roll(rows.astype(jnp.float32), acts, 1)
        from_old = jnp.where(is_act, (taken - aux) * inv_std, 0.0)
        from_new = jnp.where(is_act, (taken - head) * inv_std, 0.0)
        apart = from_old * from_old - from_new * from_new
        ratio = jnp.exp(0.5 * jnp.sum(apart, axis=1, keepdims=True))
        free = ratio * advantage
        held = jnp.clip(ratio, low, high) * advantage
        missed = head[:, acts : acts + 1] - returns
        losses = (
            -jnp.minimum(free, held)
            + (0.5 * value_coef) * missed * missed
            - entropy_coef * entropy
        )
        on_free = jnp.where(free < held, 1.0, jnp.where(free == held, 0.5, 0.0))
        inside = jnp.where(
            (ratio > low) & (ratio < high),
            1.0,
            jnp.where((ratio == low) | (ratio == high), 0.5, 0.0),
        )
        dratio = -advantage * (on_free + (1.0 - on_free) * inside)
        dlog = (factor * dratio) * ratio
        dhead = jnp.where(
            is_act,
            dlog * (from_new * inv_std),
            jnp.where(lane == acts, (factor * value_coef) * missed, 0.0),
        )
        dstd = jnp.where(is_act, -dlog * apart - factor * entropy_coef, 0.0)
        both = jnp.where(lane == acts, losses, dstd)
        totals_ref[...] += jnp.sum(both, axis=0, keepdims=True)

        dhead = dhead.astype(jnp.bfloat16)
        dnorm = dot(dhead, small_ref[:, LANES:], NT)
        dhead_ref[0:LANES, :] += dot(dhead, norm_two, TN)
        dhead_ref[LANES : LANES + 1, :] += jnp.sum(dnorm * scaled, axis=0, keepdims=True)
        dsecond = norm_backward(dnorm * gain_two, second, root_two)
        dsecond_ref[at, :] = dsecond.astype(jnp.bfloat16)
        pltpu.make_async_copy(dsecond_ref.at[at, :], dsecond_hbm.at[at, :], out_sem.at[3]).start()

    chunk = 512

    @pl.loop(0, ff // chunk)
    def _(block):
        lanes = pl.ds(pl.multiple_of(block * chunk, chunk), chunk)
        grad = dot(hidden_ref[:, lanes], dsecond_ref[...], TN)
        start = block * (chunk // 2)
        split_by_core(place_ref[0], grad, 16, keep_ref, send_ref, start, 0)
        at = pl.ds(pl.multiple_of(start, chunk // 2), chunk // 2)
        pltpu.make_async_copy(send_ref.at[at, :], send_hbm.at[at, :], out_sem.at[4]).start()

    down_out.wait()
    outs = ((pre_ref, pre_hbm), (norm_ref, norm_hbm), (dsecond_ref, dsecond_hbm))
    for place, (here, there) in enumerate(outs + ((send_ref, send_hbm),)):
        pltpu.make_async_copy(here, there, out_sem.at[place + 1]).wait()


def forward(place, rows, aux, std, weights, ff, acts, factor):
    tokens = rows.shape[0]
    group, total = weights.shape
    width = 1024
    parts = width // group
    bf16, f32 = jnp.bfloat16, jnp.float32
    shapes = [(ff // 2, width), (ff // 2, width), (tokens, ff), (tokens, width), (tokens, width), (ff, width)]
    return pl.pallas_call(
        lambda *refs: forward_kernel(acts, factor, parts, *refs),
        out_shape=tuple(jax.ShapeDtypeStruct(shape, bf16) for shape in shapes)
        + (
            jax.ShapeDtypeStruct((LANES + 8, width), f32),
            jax.ShapeDtypeStruct((1, LANES), f32),
            jax.ShapeDtypeStruct((8, width), f32),
        ),
        in_specs=[SMEM] + [VMEM] * 3 + [HBM],
        out_specs=(VMEM,) + (HBM,) * 5 + (VMEM,) * 3,
        scratch_shapes=[
            pltpu.VMEM((width, ff), bf16),
            pltpu.VMEM((width, 2 * width), bf16),
            pltpu.VMEM((width, 2 * LANES), bf16),
            pltpu.VMEM((ff, width), bf16),
            pltpu.VMEM((tokens, ff), bf16),
            pltpu.VMEM((tokens, ff), bf16),
            pltpu.VMEM((tokens, width), bf16),
            pltpu.VMEM((tokens, width), bf16),
            pltpu.VMEM((ff // 2, width), bf16),
            pltpu.SemaphoreType.DMA((3, parts)),
            pltpu.SemaphoreType.DMA((5,)),
        ],
        compiler_params=pltpu.CompilerParams(vmem_limit_bytes=VMEM_LIMIT),
        cost_estimate=pl.CostEstimate(
            flops=6 * tokens * width * ff, bytes_accessed=30 << 20, transcendentals=tokens * ff
        ),
        name="forward",
    )(place, rows, aux, std, weights)


def backward_kernel(
    heads, parts,
    place_ref, rows_ref, weights_ref, gains_ref, pre_hbm, dsecond_hbm, norm_hbm, down_hbm, dhead_ref,
    keep_ref, send_hbm,
    up_ref, win_ref, down_ref, pre_ref, dsecond_ref, norm_ref, dpre_ref, din_ref, dgain_ref, send_ref,
    in_sem, out_sem,
):
    tokens = rows_ref.shape[0]
    width, ff = up_ref.shape
    load_win = columns_in(weights_ref, parts, place_ref[1], ff + 2 * width, win_ref, in_sem.at[0])
    load_up = columns_in(weights_ref, parts, place_ref[1], 0, up_ref, in_sem.at[1])
    pairs = ((dsecond_hbm, dsecond_ref), (down_hbm, down_ref), (pre_hbm, pre_ref), (norm_hbm, norm_ref))
    loads = [
        pltpu.make_async_copy(there, here, in_sem.at[2, place])
        for place, (there, here) in enumerate(pairs)
    ]
    for copy in loads[:3] + load_win + load_up + loads[3:]:
        copy.start()
    gain_one = gains_ref[0:1, :]
    din_ref[...] = jnp.zeros_like(din_ref)
    dgain_ref[...] = jnp.zeros_like(dgain_ref)
    for copy in loads[:3]:
        copy.wait()

    @pl.loop(0, tokens // TOKEN_BLOCK)
    def _(block):
        at = pl.ds(pl.multiple_of(block * TOKEN_BLOCK, TOKEN_BLOCK), TOKEN_BLOCK)
        dsecond = dsecond_ref[at, :]
        chunk = 1024
        for start in range(0, ff, chunk):
            lanes = slice(start, start + chunk)
            dhidden = dot(dsecond, down_ref[lanes, :], NT)
            pre = pre_ref[at, lanes].astype(jnp.float32)
            square = pre * pre
            bent = jnp.tanh(pre * (GELU_RATE + GELU_CUBE * square))
            half = 0.5 * pre
            slope = 0.5 + 0.5 * bent + (half - half * (bent * bent)) * (
                GELU_RATE + (3.0 * GELU_CUBE) * square
            )
            dpre_ref[at, lanes] = (dhidden * slope).astype(jnp.bfloat16)

    for copy in load_win + load_up:
        copy.wait()

    @pl.loop(0, tokens // TOKEN_BLOCK)
    def _(block):
        at = pl.ds(pl.multiple_of(block * TOKEN_BLOCK, TOKEN_BLOCK), TOKEN_BLOCK)
        rows = rows_ref[at, :]
        first = dot(rows, win_ref[...], NT)
        root = mean_square_root(first)
        dnorm = dot(dpre_ref[at, :], up_ref[...], NT)
        dgain_ref[0:1, :] += jnp.sum(dnorm * (first * root), axis=0, keepdims=True)
        dfirst = dsecond_ref[at, :].astype(jnp.float32)
        dfirst = dfirst + norm_backward(dnorm * gain_one, first, root)
        din_ref[...] += dot(rows, dfirst.astype(jnp.bfloat16), TN)

    loads[3].wait()
    chunk = 512
    ids = lax.broadcasted_iota(jnp.int32, (LANES, chunk), 0)

    @pl.loop(0, width // chunk)
    def _(block):
        lanes = pl.ds(pl.multiple_of(block * chunk, chunk), chunk)
        core = place_ref[0]
        half = block * (chunk // 2)
        for start in range(0, ff, 1024):
            grad = dot(norm_ref[:, lanes], dpre_ref[:, start : start + 1024], TN)
            split_by_core(core, grad, 8, keep_ref, send_ref, half, start)
        split_by_core(core, jnp.transpose(din_ref[:, lanes]), 8, keep_ref, send_ref, half, ff)
        tail = jnp.where(ids == heads, dgain_ref[0:1, lanes], dhead_ref[0:LANES, lanes])
        tail = jnp.where(ids == heads + 1, dhead_ref[LANES : LANES + 1, lanes], tail)
        split_by_core(core, jnp.transpose(tail), 8, keep_ref, send_ref, half, ff + LANES)
        at = pl.ds(pl.multiple_of(half, chunk // 2), chunk // 2)
        pltpu.make_async_copy(send_ref.at[at, :], send_hbm.at[at, :], out_sem).start()

    pltpu.make_async_copy(send_ref, send_hbm, out_sem).wait()


def backward(heads, place, rows, weights, gains, pre, dsecond, norm_one, down, dhead):
    tokens, ff = pre.shape
    width = dsecond.shape[1]
    parts = width // weights.shape[0]
    bf16, f32 = jnp.bfloat16, jnp.float32
    out = jax.ShapeDtypeStruct((width // 2, ff + 2 * LANES), bf16)
    return pl.pallas_call(
        lambda *refs: backward_kernel(heads, parts, *refs),
        out_shape=(out, out),
        in_specs=[SMEM, VMEM, HBM, VMEM] + [HBM] * 4 + [VMEM],
        out_specs=(VMEM, HBM),
        scratch_shapes=[
            pltpu.VMEM((width, ff), bf16),
            pltpu.VMEM((width, LANES), bf16),
            pltpu.VMEM((ff, width), bf16),
            pltpu.VMEM((tokens, ff), bf16),
            pltpu.VMEM((tokens, width), bf16),
            pltpu.VMEM((tokens, width), bf16),
            pltpu.VMEM((tokens, ff), bf16),
            pltpu.VMEM((LANES, width), f32),
            pltpu.VMEM((8, width), f32),
            pltpu.VMEM(out.shape, bf16),
            pltpu.SemaphoreType.DMA((3, max(parts, 4))),
            pltpu.SemaphoreType.DMA,
        ],
        compiler_params=pltpu.CompilerParams(vmem_limit_bytes=VMEM_LIMIT),
        cost_estimate=pl.CostEstimate(
            flops=6 * tokens * width * ff, bytes_accessed=30 << 20, transcendentals=tokens * ff
        ),
        name="backward",
    )(place, rows, weights, gains, pre, dsecond, norm_one, down, dhead)


def pair_kernel(keep_ref, came_ref, out_ref):
    many = keep_ref.shape[0] // 4

    @pl.loop(0, 4)
    def _(block):
        at = pl.ds(pl.multiple_of(block * many, many), many)
        total = keep_ref[at, :].astype(jnp.float32) + came_ref[at, :].astype(jnp.float32)
        out_ref[at, :] = total.astype(jnp.bfloat16)


def pair_totals_kernel(place, count, rows, mine_ref, other_ref, keep_ref, came_ref, out_ref):
    f32, bf16 = jnp.float32, jnp.bfloat16
    cut = keep_ref.shape[1] - LANES
    pair_kernel(keep_ref.at[:, :cut], came_ref.at[:, :cut], out_ref.at[:, :cut])
    lane = lax.broadcasted_iota(jnp.int32, (8, LANES), 1)
    totals = jnp.broadcast_to(mine_ref[...] + other_ref[...], (8, LANES))
    totals = jnp.where(lane < count, totals, 0.0)
    first = totals.astype(bf16).astype(f32)
    second = (totals - first).astype(bf16).astype(f32)
    third = totals - first - second
    line = (
        pltpu.roll(first, place, 1)
        + pltpu.roll(second, place + count, 1)
        + pltpu.roll(third, place + 2 * count, 1)
    )
    tail = keep_ref[:, cut:].astype(f32) + came_ref[:, cut:].astype(f32)
    row = lax.broadcasted_iota(jnp.int32, tail.shape, 0) % rows
    lane = lax.broadcasted_iota(jnp.int32, tail.shape, 1)
    special = (row == 0) & (lane >= place) & (lane < place + 3 * count)
    out_ref[:, cut:] = jnp.where(special, line[0:1], tail).astype(bf16)


def pair_sum(keep, came, kernel=pair_kernel, small=()):
    return pl.pallas_call(
        kernel,
        out_shape=jax.ShapeDtypeStruct(keep.shape, keep.dtype),
        in_specs=[VMEM] * (len(small) + 2),
        out_specs=VMEM,
        compiler_params=pltpu.CompilerParams(vmem_limit_bytes=VMEM_LIMIT // 3),
        name="pair",
    )(*small, keep, came)


def finish_kernel(
    acts, came_ref, in_ref, one_ref, up_ref, two_ref, head_ref, std_ref, loss_ref
):
    ff = up_ref.shape[1]
    obs = in_ref.shape[1]
    heads = head_ref.shape[1]
    total = came_ref[0].astype(jnp.float32)
    for chip in range(1, came_ref.shape[0]):
        total = total + came_ref[chip].astype(jnp.float32)
    up_ref[...] = total[:, :ff]
    in_ref[...] = total[:, ff : ff + obs]
    tail = total[:, ff + LANES :]
    head_ref[...] = tail[:, :heads]
    flipped = jnp.transpose(tail)
    one_ref[...] = flipped[heads : heads + 1]
    two_ref[...] = flipped[heads + 1 : heads + 2]
    count = acts + 1
    place = heads + 2
    whole = (
        pltpu.roll(tail, LANES - place, 1)
        + pltpu.roll(tail, LANES - place - count, 1)
        + pltpu.roll(tail, LANES - place - 2 * count, 1)
    )[0:1]
    std_ref[...] = whole[:, :acts]
    loss_ref[...] = whole[:, acts : acts + 1]


def finish(came, ff, obs, heads, acts):
    rows = came.shape[1]
    shapes = ((rows, obs), (1, rows), (rows, ff), (1, rows), (rows, heads), (1, acts), (1, 1))
    return pl.pallas_call(
        lambda *refs: finish_kernel(acts, *refs),
        out_shape=tuple(jax.ShapeDtypeStruct(shape, jnp.float32) for shape in shapes),
        in_specs=[VMEM],
        out_specs=(VMEM,) * 7,
        compiler_params=pltpu.CompilerParams(vmem_limit_bytes=VMEM_LIMIT // 3),
        name="finish",
    )(came)


def lanes_of(*columns):
    filled = sum(c.shape[1] for c in columns)
    gap = jnp.zeros((columns[0].shape[0], LANES - filled), columns[0].dtype)
    return jnp.concatenate(columns + (gap,), axis=1)


def body(
    q_start, v_start, minv, geom_jac, pairs, gap_start, actions, act_map, batch_index,
    w_in, gain_one, w_up, w_down, gain_two, w_head, log_std, old_mu, advantage, returns,
):
    count = lax.axis_size(EVERY)
    chips = count // 2
    rows_up, ff = w_up.shape
    rows_down, width = w_down.shape
    obs = w_in.shape[0]
    heads = w_head.shape[1]
    acts = log_std.shape[0]
    per_peer = batch_index.shape[2]
    tokens = old_mu.shape[0]
    place = jnp.stack([lax.axis_index("c"), lax.axis_index("x")]).astype(jnp.int32)

    packed = pack(
        w_up, w_down, jnp.transpose(w_in), w_head, gain_one.reshape(1, -1), gain_two.reshape(1, -1)
    )
    beside = [packed]
    for step in (1, 2, 3):
        beside.append(lax.ppermute(packed, "x", [((i + step) % 4, i) for i in range(4)]))
    ordered = jnp.concatenate(beside, axis=1)
    weights = lax.all_gather(ordered, ("z", "y", "c"), axis=0, tiled=True)

    picks = batch_index.reshape(1, count * per_peer)
    q_final, v_final, picked = rollout(
        q_start, v_start, minv, geom_jac, pairs, gap_start, actions, act_map, picks
    )
    row_width = picked.shape[1]
    arrived = lax.all_to_all(
        picked.reshape(count, per_peer, row_width), EVERY, split_axis=0, concat_axis=0, tiled=True
    )
    rows = arrived.reshape(tokens, row_width)
    aux = lanes_of(old_mu, advantage[:, None], returns[:, None])
    std = lanes_of(log_std[None])

    factor = loss_scale / (tokens * count)
    keep, send, pre, dsecond, norm_one, down, dhead, totals, gain_rows = forward(
        place, rows, aux, std, weights, ff, acts, factor
    )

    pair = pair_sum(keep, lax.ppermute(send, "c", SWAP))
    pair, dsecond = lax.optimization_barrier((pair, dsecond))
    down_came = lax.all_to_all(
        pair.reshape(chips, rows_down, width), WIRE, split_axis=0, concat_axis=0, tiled=True
    )
    other_totals = lax.ppermute(totals, "c", SWAP)
    keep, send = backward(
        heads, place, rows, weights, gain_rows, pre, dsecond, norm_one, down, dhead
    )
    send, down_came = lax.optimization_barrier((send, down_came))
    grad_down = jnp.sum(down_came.astype(jnp.float32), axis=0)

    pair = pair_sum(
        keep,
        lax.ppermute(send, "c", SWAP),
        lambda *refs: pair_totals_kernel(heads + 2, acts + 1, rows_up, *refs),
        (totals, other_totals),
    )
    up_came = lax.all_to_all(
        pair.reshape(chips, rows_up, -1), WIRE, split_axis=0, concat_axis=0, tiled=True
    )
    grad_in, grad_one, grad_up, grad_two, grad_head, grad_std, loss = finish(
        up_came, ff, obs, heads, acts
    )
    return (
        q_final,
        v_final,
        jnp.transpose(grad_in),
        grad_one.reshape(-1),
        grad_up,
        grad_down,
        grad_two.reshape(-1),
        grad_head,
        grad_std.reshape(-1),
        loss.reshape(()) / (tokens * count),
    )


def solution(mesh):
    grid = Mesh(mesh.devices.reshape(4, 4, 4, 2), EVERY)
    placed = (
        P(None, EVERY),
        P(None, EVERY),
        P(None, None, EVERY),
        P(None, None, EVERY),
        P(None, None, EVERY),
        P(None, EVERY),
        P(None, None, EVERY),
        P(),
        P(EVERY, None, None),
        P(None, EVERY),
        P(EVERY),
        P(EVERY, None),
        P(EVERY, None),
        P(EVERY),
        P(EVERY, None),
        P(),
        P(EVERY, None),
        P(EVERY),
        P(EVERY),
    )
    return jax.shard_map(
        body,
        mesh=grid,
        in_specs=placed,
        out_specs=(
            P(None, EVERY),
            P(None, EVERY),
            P(None, EVERY),
            P(EVERY),
            P(EVERY, None),
            P(EVERY, None),
            P(EVERY),
            P(EVERY, None),
            P(),
            P(),
        ),
        check_vma=False,
    )
```

```python
import math

import jax
import jax.numpy as jnp
from jax import lax
from jax.experimental import pallas as pl
from jax.experimental.pallas import tpu as pltpu
from jax.sharding import Mesh
from jax.sharding import PartitionSpec as P

EVERY = ("x", "z", "y", "c")
WIRE = ("x", "z", "y")
LANES = 128
SWAP = [(0, 1), (1, 0)]
VMEM_LIMIT = 46 * 1024 * 1024

BINS = 32
ITERS = 8
time_step = 0.02
damping = 0.5
torque = 2.0
baumgarte = 0.2
soft_reg = 0.1
clip_eps = 0.2
value_coef = 0.5
entropy_coef = 0.01
loss_scale = 1024.0

VMEM = pl.BlockSpec(memory_space=pltpu.VMEM)
SMEM = pl.BlockSpec(memory_space=pltpu.SMEM)


def dot(a, b, dims, precision=None):
    return lax.dot_general(
        a, b, (dims, ((), ())), precision=precision, preferred_element_type=jnp.float32
    )


NN = ((1,), (0,))
NT = ((1,), (1,))
TN = ((0,), (0,))


def spread(row, rows):
    return jnp.broadcast_to(row, (rows, row.shape[-1]))


def rollout_kernel(
    q_ref, v_ref, minv_ref, geom_ref, pairs_ref, gap_ref, act_ref, map_ref, picks_ref,
    q_out, v_out, rows_out,
    select, jac, mob, dela, stored,
):
    geoms, dof, envs = geom_ref.shape
    cont = gap_ref.shape[0]
    steps, acts, _ = act_ref.shape

    @pl.loop(0, geoms)
    def _(g):
        first = (pairs_ref[0] == g).astype(jnp.float32)
        select[g] = first - (pairs_ref[1] == g).astype(jnp.float32)

    def by_rows(count, many, depth, left, right, out):
        @pl.loop(0, count // many)
        def _(block):
            sums = [jnp.zeros((cont, envs), jnp.float32) for _ in range(many)]
            for k in range(depth):
                held = right(k)
                for i in range(many):
                    sums[i] = sums[i] + spread(left(k, block * many + i), cont) * held
            for i in range(many):
                out[block * many + i] = sums[i]

    by_rows(dof, 3, geoms, lambda g, d: geom_ref[g, pl.ds(d, 1), :], lambda g: select[g], jac)
    by_rows(dof, 3, dof, lambda k, d: minv_ref[d, pl.ds(k, 1), :], lambda k: jac[k], mob)
    by_rows(cont, 4, dof, lambda d, e: mob[d, pl.ds(e, 1), :], lambda d: jac[d], dela)

    denom = jnp.full((cont, envs), soft_reg, jnp.float32)
    for e in range(cont):
        denom = denom + jnp.abs(dela[e])
    inverse = 1.0 / denom
    gap_rate = baumgarte / time_step
    q_first = q_ref[...]
    gap_first = gap_ref[...] * gap_rate

    def one_step(s, carry):
        q, v, lam = carry
        level = act_ref[s].astype(jnp.float32) * (2.0 / (BINS - 1)) - 1.0
        force = torque * dot(map_ref[...], level, NN, lax.Precision.HIGHEST) - damping * v
        pushed = jnp.zeros_like(v)
        for k in range(dof):
            pushed = pushed + minv_ref[k] * spread(force[k : k + 1], dof)
        vfree = v + time_step * pushed
        drift = vfree + gap_rate * (q - q_first)
        bias = gap_first
        for d in range(dof):
            bias = bias + jac[d] * spread(drift[d : d + 1], cont)

        def sweep(_, lam):
            push = [bias, jnp.zeros_like(bias)]
            for e in range(cont):
                push[e % 2] = push[e % 2] + dela[e] * spread(lam[e : e + 1], cont)
            return jnp.maximum(lam - (push[0] + push[1]) * inverse, 0.0)

        lam = lax.fori_loop(0, ITERS, sweep, lam)
        gained = [jnp.sum(mob[d] * lam, axis=0, keepdims=True) for d in range(dof)]
        v = vfree + jnp.concatenate(gained, axis=0)
        q = q + time_step * v
        stored[s] = jnp.concatenate([q, v, lam, level], axis=0).astype(jnp.bfloat16)
        return q, v, lam

    q, v, _ = lax.fori_loop(
        0, steps, one_step, (q_first, v_ref[...], jnp.zeros((cont, envs), jnp.float32))
    )
    q_out[...] = q
    v_out[...] = v

    picks = picks_ref.shape[1]
    block = 256
    for start in range(0, picks, block):
        wanted = picks_ref[:, start : start + block]
        found = jnp.zeros((stored.shape[1], block), jnp.float32)
        for s in range(steps):
            ids = lax.broadcasted_iota(jnp.int32, (envs, block), 0) + s * envs
            hit = (ids == wanted).astype(jnp.float32).astype(jnp.bfloat16)
            found = found + dot(stored[s], hit, NN)
        rows_out[start : start + block, :] = jnp.transpose(found).astype(jnp.bfloat16)


def rollout(q_start, v_start, minv, geom_jac, pairs, gap_start, actions, act_map, picks):
    geoms, dof, envs = geom_jac.shape
    cont = gap_start.shape[0]
    steps, acts, _ = actions.shape
    row = 2 * dof + cont + acts
    return pl.pallas_call(
        rollout_kernel,
        out_shape=(
            jax.ShapeDtypeStruct((dof, envs), jnp.float32),
            jax.ShapeDtypeStruct((dof, envs), jnp.float32),
            jax.ShapeDtypeStruct((picks.shape[1], row), jnp.bfloat16),
        ),
        in_specs=[VMEM] * 9,
        out_specs=(VMEM,) * 3,
        scratch_shapes=[
            pltpu.VMEM((geoms, cont, envs), jnp.float32),
            pltpu.VMEM((dof, cont, envs), jnp.float32),
            pltpu.VMEM((dof, cont, envs), jnp.float32),
            pltpu.VMEM((cont, cont, envs), jnp.float32),
            pltpu.VMEM((steps, row, envs), jnp.bfloat16),
        ],
        compiler_params=pltpu.CompilerParams(vmem_limit_bytes=VMEM_LIMIT),
        name="rollout",
    )(q_start, v_start, minv, geom_jac, pairs, gap_start, actions, act_map, picks)


TOKEN_BLOCK = 512
HBM = pl.BlockSpec(memory_space=pl.ANY)
GELU_RATE = math.sqrt(2.0 / math.pi)
GELU_CUBE = 0.044715 * GELU_RATE


def mean_square_root(values):
    return lax.rsqrt(jnp.mean(values * values, axis=1, keepdims=True) + 1e-05)


def norm_backward(grad, values, root):
    inner = jnp.mean(grad * values, axis=1, keepdims=True)
    return root * (grad - values * (root * root * inner))


def split_by_core(core, block, rows, keep_ref, send_ref, start, lane):
    count, columns = block.shape
    groups = block.reshape(count // (2 * rows), 2, rows, columns)
    half = count // 2
    at = pl.ds(pl.multiple_of(start, half), half)
    lanes = slice(lane, lane + columns)
    for which in range(2):
        part = groups[:, which].reshape(half, columns).astype(jnp.bfloat16)

        @pl.when(core == which)
        def _():
            keep_ref[at, lanes] = part

        @pl.when(core != which)
        def _():
            send_ref[at, lanes] = part


def pack_kernel(up_ref, down_ref, in_ref, head_ref, one_ref, two_ref, out_ref):
    rows, ff = up_ref.shape
    width = down_ref.shape[1]
    obs = in_ref.shape[1]
    heads = head_ref.shape[1]
    f32 = jnp.float32
    out_ref[:, :ff] = up_ref[...]
    down = down_ref[...].astype(f32)
    out_ref[:, ff : ff + width] = down[:rows].astype(jnp.bfloat16)
    out_ref[:, ff + width : ff + 2 * width] = down[rows:].astype(jnp.bfloat16)
    first = jnp.concatenate(
        [in_ref[...].astype(f32), jnp.zeros((rows, LANES - obs), f32)], axis=1
    )
    gains = jnp.concatenate(
        [one_ref[...].astype(f32), two_ref[...].astype(f32), jnp.zeros((LANES - 2, rows), f32)],
        axis=0,
    )
    second = pltpu.roll(jnp.transpose(gains), heads, 1)
    wide = jnp.concatenate(
        [head_ref[...].astype(f32), jnp.zeros((rows, LANES - heads), f32)], axis=1
    )
    both = jnp.concatenate([first, second + wide], axis=1)
    out_ref[:, ff + 2 * width :] = both.astype(jnp.bfloat16)


def pack(w_up, w_down, w_in, w_head, gain_one, gain_two):
    rows, ff = w_up.shape
    width = w_down.shape[1]
    return pl.pallas_call(
        pack_kernel,
        out_shape=jax.ShapeDtypeStruct((rows, ff + 2 * width + 2 * LANES), jnp.bfloat16),
        in_specs=[VMEM] * 6,
        out_specs=VMEM,
        name="pack",
    )(w_up, w_down, w_in, w_head, gain_one, gain_two)


def columns_in(weights_ref, parts, first, start, out_ref, sem):
    rows, total = weights_ref.shape
    columns = out_ref.shape[1]
    each = total // parts
    return [
        pltpu.make_async_copy(
            weights_ref.at[:, pl.ds(part * each + start, columns)],
            out_ref.at[pl.ds(pl.multiple_of((first + part) % parts * rows, rows), rows), :],
            sem.at[part],
        )
        for part in range(parts)
    ]


def forward_kernel(
    acts, factor, parts,
    place_ref, rows_ref, aux_ref, std_ref, weights_ref,
    keep_ref, send_hbm, pre_hbm, dsecond_hbm, norm_hbm, down_hbm, dhead_ref, totals_ref, gains_ref,
    up_ref, both_ref, small_ref, down_ref, hidden_ref, pre_ref, dsecond_ref, norm_ref, send_ref,
    in_sem, out_sem,
):
    tokens = rows_ref.shape[0]
    width, ff = up_ref.shape
    load_small = columns_in(weights_ref, parts, place_ref[1], ff + 2 * width, small_ref, in_sem.at[0])
    load_up = columns_in(weights_ref, parts, place_ref[1], 0, up_ref, in_sem.at[1])
    load_both = columns_in(weights_ref, parts, place_ref[1], ff, both_ref, in_sem.at[2])
    for copy in load_small + load_both + load_up:
        copy.start()

    inv_std = jnp.exp(-std_ref[...])
    lane = lax.broadcasted_iota(jnp.int32, (1, LANES), 1)
    is_act = lane < acts
    entropy = jnp.sum(jnp.where(is_act, std_ref[...], 0.0)) + 0.5 * acts * (
        1.0 + math.log(2.0 * math.pi)
    )
    dhead_ref[...] = jnp.zeros_like(dhead_ref)
    totals_ref[...] = jnp.zeros_like(totals_ref)
    low, high = 1.0 - clip_eps, 1.0 + clip_eps

    for copy in load_small:
        copy.wait()
    gains_ref[...] = jnp.transpose(small_ref[:, LANES:].astype(jnp.float32))[acts + 1 : acts + 9]
    gain_one = gains_ref[0:1, :]
    gain_two = gains_ref[1:2, :]

    many = 128
    for part, copy in enumerate(load_both):
        copy.wait()

        @pl.loop(0, width // parts // many)
        def _(step):
            block = (place_ref[1] + part) % parts * (width // parts // many) + step
            at = pl.ds(pl.multiple_of(block * many, many), many)
            halves = both_ref[at, :].astype(jnp.float32).reshape(many // 8, 8, 2 * width)
            mixed = jnp.stack([halves[:, :, :width], halves[:, :, width:]], axis=1)
            to = pl.ds(pl.multiple_of(block * 2 * many, 2 * many), 2 * many)
            down_ref[to, :] = mixed.reshape(2 * many, width).astype(jnp.bfloat16)

    down_out = pltpu.make_async_copy(down_ref, down_hbm, out_sem.at[0])
    down_out.start()
    for copy in load_up:
        copy.wait()

    @pl.loop(0, tokens // TOKEN_BLOCK)
    def _(block):
        at = pl.ds(pl.multiple_of(block * TOKEN_BLOCK, TOKEN_BLOCK), TOKEN_BLOCK)
        rows = rows_ref[at, :]
        first = dot(rows, small_ref[:, :LANES], NT)
        norm_one = (first * mean_square_root(first) * gain_one).astype(jnp.bfloat16)
        norm_ref[at, :] = norm_one
        second = first
        chunk = 1024
        for start in range(0, ff, chunk):
            lanes = slice(start, start + chunk)
            pre = dot(norm_one, up_ref[:, lanes], NN)
            pre_ref[at, lanes] = pre.astype(jnp.bfloat16)
            bent = jnp.tanh(pre * (GELU_RATE + GELU_CUBE * (pre * pre)))
            half = 0.5 * pre
            hidden = (half + half * bent).astype(jnp.bfloat16)
            hidden_ref[at, lanes] = hidden
            second = second + dot(hidden, down_ref[lanes, :], NN)
        pltpu.make_async_copy(pre_ref.at[at, :], pre_hbm.at[at, :], out_sem.at[1]).start()
        pltpu.make_async_copy(norm_ref.at[at, :], norm_hbm.at[at, :], out_sem.at[2]).start()
        root_two = mean_square_root(second)
        scaled = second * root_two
        norm_two = (scaled * gain_two).astype(jnp.bfloat16)
        head = dot(norm_two, small_ref[:, LANES:], NN)

        aux = aux_ref[at, :]
        advantage = aux[:, acts : acts + 1]
        returns = aux[:, acts + 1 : acts + 2]
        taken = pltpu.roll(rows.astype(jnp.float32), acts, 1)
        from_old = jnp.where(is_act, (taken - aux) * inv_std, 0.0)
        from_new = jnp.where(is_act, (taken - head) * inv_std, 0.0)
        apart = from_old * from_old - from_new * from_new
        ratio = jnp.exp(0.5 * jnp.sum(apart, axis=1, keepdims=True))
        free = ratio * advantage
        held = jnp.clip(ratio, low, high) * advantage
        missed = head[:, acts : acts + 1] - returns
        losses = (
            -jnp.minimum(free, held)
            + (0.5 * value_coef) * missed * missed
            - entropy_coef * entropy
        )
        on_free = jnp.where(free < held, 1.0, jnp.where(free == held, 0.5, 0.0))
        inside = jnp.where(
            (ratio > low) & (ratio < high),
            1.0,
            jnp.where((ratio == low) | (ratio == high), 0.5, 0.0),
        )
        dratio = -advantage * (on_free + (1.0 - on_free) * inside)
        dlog = (factor * dratio) * ratio
        dhead = jnp.where(
            is_act,
            dlog * (from_new * inv_std),
            jnp.where(lane == acts, (factor * value_coef) * missed, 0.0),
        )
        dstd = jnp.where(is_act, -dlog * apart - factor * entropy_coef, 0.0)
        both = jnp.where(lane == acts, losses, dstd)
        totals_ref[...] += jnp.sum(both, axis=0, keepdims=True)

        dhead = dhead.astype(jnp.bfloat16)
        dnorm = dot(dhead, small_ref[:, LANES:], NT)
        dhead_ref[0:LANES, :] += dot(dhead, norm_two, TN)
        dhead_ref[LANES : LANES + 1, :] += jnp.sum(dnorm * scaled, axis=0, keepdims=True)
        dsecond = norm_backward(dnorm * gain_two, second, root_two)
        dsecond_ref[at, :] = dsecond.astype(jnp.bfloat16)
        pltpu.make_async_copy(dsecond_ref.at[at, :], dsecond_hbm.at[at, :], out_sem.at[3]).start()

    chunk = 512

    @pl.loop(0, ff // chunk)
    def _(block):
        lanes = pl.ds(pl.multiple_of(block * chunk, chunk), chunk)
        grad = dot(hidden_ref[:, lanes], dsecond_ref[...], TN)
        start = block * (chunk // 2)
        split_by_core(place_ref[0], grad, 16, keep_ref, send_ref, start, 0)
        at = pl.ds(pl.multiple_of(start, chunk // 2), chunk // 2)
        pltpu.make_async_copy(send_ref.at[at, :], send_hbm.at[at, :], out_sem.at[4]).start()

    down_out.wait()
    outs = ((pre_ref, pre_hbm), (norm_ref, norm_hbm), (dsecond_ref, dsecond_hbm))
    for place, (here, there) in enumerate(outs + ((send_ref, send_hbm),)):
        pltpu.make_async_copy(here, there, out_sem.at[place + 1]).wait()


def forward(place, rows, aux, std, weights, ff, acts, factor):
    tokens = rows.shape[0]
    group, total = weights.shape
    width = 1024
    parts = width // group
    bf16, f32 = jnp.bfloat16, jnp.float32
    shapes = [(ff // 2, width), (ff // 2, width), (tokens, ff), (tokens, width), (tokens, width), (ff, width)]
    return pl.pallas_call(
        lambda *refs: forward_kernel(acts, factor, parts, *refs),
        out_shape=tuple(jax.ShapeDtypeStruct(shape, bf16) for shape in shapes)
        + (
            jax.ShapeDtypeStruct((LANES + 8, width), f32),
            jax.ShapeDtypeStruct((1, LANES), f32),
            jax.ShapeDtypeStruct((8, width), f32),
        ),
        in_specs=[SMEM] + [VMEM] * 3 + [HBM],
        out_specs=(VMEM,) + (HBM,) * 5 + (VMEM,) * 3,
        scratch_shapes=[
            pltpu.VMEM((width, ff), bf16),
            pltpu.VMEM((width, 2 * width), bf16),
            pltpu.VMEM((width, 2 * LANES), bf16),
            pltpu.VMEM((ff, width), bf16),
            pltpu.VMEM((tokens, ff), bf16),
            pltpu.VMEM((tokens, ff), bf16),
            pltpu.VMEM((tokens, width), bf16),
            pltpu.VMEM((tokens, width), bf16),
            pltpu.VMEM((ff // 2, width), bf16),
            pltpu.SemaphoreType.DMA((3, parts)),
            pltpu.SemaphoreType.DMA((5,)),
        ],
        compiler_params=pltpu.CompilerParams(vmem_limit_bytes=VMEM_LIMIT),
        cost_estimate=pl.CostEstimate(
            flops=6 * tokens * width * ff, bytes_accessed=30 << 20, transcendentals=tokens * ff
        ),
        name="forward",
    )(place, rows, aux, std, weights)


def backward_kernel(
    heads, parts,
    place_ref, rows_ref, weights_ref, gains_ref, pre_hbm, dsecond_hbm, norm_hbm, down_hbm, dhead_ref,
    keep_ref, send_hbm,
    up_ref, win_ref, down_ref, pre_ref, dsecond_ref, norm_ref, dpre_ref, din_ref, dgain_ref, send_ref,
    in_sem, out_sem,
):
    tokens = rows_ref.shape[0]
    width, ff = up_ref.shape
    load_win = columns_in(weights_ref, parts, place_ref[1], ff + 2 * width, win_ref, in_sem.at[0])
    load_up = columns_in(weights_ref, parts, place_ref[1], 0, up_ref, in_sem.at[1])
    pairs = ((dsecond_hbm, dsecond_ref), (down_hbm, down_ref), (pre_hbm, pre_ref), (norm_hbm, norm_ref))
    loads = [
        pltpu.make_async_copy(there, here, in_sem.at[2, place])
        for place, (there, here) in enumerate(pairs)
    ]
    for copy in loads[:3] + load_win + load_up + loads[3:]:
        copy.start()
    gain_one = gains_ref[0:1, :]
    din_ref[...] = jnp.zeros_like(din_ref)
    dgain_ref[...] = jnp.zeros_like(dgain_ref)
    for copy in loads[:3]:
        copy.wait()

    @pl.loop(0, tokens // TOKEN_BLOCK)
    def _(block):
        at = pl.ds(pl.multiple_of(block * TOKEN_BLOCK, TOKEN_BLOCK), TOKEN_BLOCK)
        dsecond = dsecond_ref[at, :]
        chunk = 1024
        for start in range(0, ff, chunk):
            lanes = slice(start, start + chunk)
            dhidden = dot(dsecond, down_ref[lanes, :], NT)
            pre = pre_ref[at, lanes].astype(jnp.float32)
            square = pre * pre
            bent = jnp.tanh(pre * (GELU_RATE + GELU_CUBE * square))
            half = 0.5 * pre
            slope = 0.5 + 0.5 * bent + (half - half * (bent * bent)) * (
                GELU_RATE + (3.0 * GELU_CUBE) * square
            )
            dpre_ref[at, lanes] = (dhidden * slope).astype(jnp.bfloat16)

    for copy in load_win + load_up:
        copy.wait()

    @pl.loop(0, tokens // TOKEN_BLOCK)
    def _(block):
        at = pl.ds(pl.multiple_of(block * TOKEN_BLOCK, TOKEN_BLOCK), TOKEN_BLOCK)
        rows = rows_ref[at, :]
        first = dot(rows, win_ref[...], NT)
        root = mean_square_root(first)
        dnorm = dot(dpre_ref[at, :], up_ref[...], NT)
        dgain_ref[0:1, :] += jnp.sum(dnorm * (first * root), axis=0, keepdims=True)
        dfirst = dsecond_ref[at, :].astype(jnp.float32)
        dfirst = dfirst + norm_backward(dnorm * gain_one, first, root)
        din_ref[...] += dot(rows, dfirst.astype(jnp.bfloat16), TN)

    loads[3].wait()
    chunk = 512
    ids = lax.broadcasted_iota(jnp.int32, (LANES, chunk), 0)

    @pl.loop(0, width // chunk)
    def _(block):
        lanes = pl.ds(pl.multiple_of(block * chunk, chunk), chunk)
        core = place_ref[0]
        half = block * (chunk // 2)
        for start in range(0, ff, 1024):
            grad = dot(norm_ref[:, lanes], dpre_ref[:, start : start + 1024], TN)
            split_by_core(core, grad, 8, keep_ref, send_ref, half, start)
        split_by_core(core, jnp.transpose(din_ref[:, lanes]), 8, keep_ref, send_ref, half, ff)
        tail = jnp.where(ids == heads, dgain_ref[0:1, lanes], dhead_ref[0:LANES, lanes])
        tail = jnp.where(ids == heads + 1, dhead_ref[LANES : LANES + 1, lanes], tail)
        split_by_core(core, jnp.transpose(tail), 8, keep_ref, send_ref, half, ff + LANES)
        at = pl.ds(pl.multiple_of(half, chunk // 2), chunk // 2)
        pltpu.make_async_copy(send_ref.at[at, :], send_hbm.at[at, :], out_sem).start()

    pltpu.make_async_copy(send_ref, send_hbm, out_sem).wait()


def backward(heads, place, rows, weights, gains, pre, dsecond, norm_one, down, dhead):
    tokens, ff = pre.shape
    width = dsecond.shape[1]
    parts = width // weights.shape[0]
    bf16, f32 = jnp.bfloat16, jnp.float32
    out = jax.ShapeDtypeStruct((width // 2, ff + 2 * LANES), bf16)
    return pl.pallas_call(
        lambda *refs: backward_kernel(heads, parts, *refs),
        out_shape=(out, out),
        in_specs=[SMEM, VMEM, HBM, VMEM] + [HBM] * 4 + [VMEM],
        out_specs=(VMEM, HBM),
        scratch_shapes=[
            pltpu.VMEM((width, ff), bf16),
            pltpu.VMEM((width, LANES), bf16),
            pltpu.VMEM((ff, width), bf16),
            pltpu.VMEM((tokens, ff), bf16),
            pltpu.VMEM((tokens, width), bf16),
            pltpu.VMEM((tokens, width), bf16),
            pltpu.VMEM((tokens, ff), bf16),
            pltpu.VMEM((LANES, width), f32),
            pltpu.VMEM((8, width), f32),
            pltpu.VMEM(out.shape, bf16),
            pltpu.SemaphoreType.DMA((3, max(parts, 4))),
            pltpu.SemaphoreType.DMA,
        ],
        compiler_params=pltpu.CompilerParams(vmem_limit_bytes=58 * 1024 * 1024),
        cost_estimate=pl.CostEstimate(
            flops=6 * tokens * width * ff, bytes_accessed=30 << 20, transcendentals=tokens * ff
        ),
        name="backward",
    )(place, rows, weights, gains, pre, dsecond, norm_one, down, dhead)


def pair_kernel(keep_ref, came_ref, out_ref):
    many = keep_ref.shape[0] // 4

    @pl.loop(0, 4)
    def _(block):
        at = pl.ds(pl.multiple_of(block * many, many), many)
        total = keep_ref[at, :].astype(jnp.float32) + came_ref[at, :].astype(jnp.float32)
        out_ref[at, :] = total.astype(jnp.bfloat16)


def pair_totals_kernel(place, count, rows, mine_ref, other_ref, keep_ref, came_ref, out_ref):
    f32, bf16 = jnp.float32, jnp.bfloat16
    cut = keep_ref.shape[1] - LANES
    pair_kernel(keep_ref.at[:, :cut], came_ref.at[:, :cut], out_ref.at[:, :cut])
    lane = lax.broadcasted_iota(jnp.int32, (8, LANES), 1)
    totals = jnp.broadcast_to(mine_ref[...] + other_ref[...], (8, LANES))
    totals = jnp.where(lane < count, totals, 0.0)
    first = totals.astype(bf16).astype(f32)
    second = (totals - first).astype(bf16).astype(f32)
    third = totals - first - second
    line = (
        pltpu.roll(first, place, 1)
        + pltpu.roll(second, place + count, 1)
        + pltpu.roll(third, place + 2 * count, 1)
    )
    tail = keep_ref[:, cut:].astype(f32) + came_ref[:, cut:].astype(f32)
    row = lax.broadcasted_iota(jnp.int32, tail.shape, 0) % rows
    lane = lax.broadcasted_iota(jnp.int32, tail.shape, 1)
    special = (row == 0) & (lane >= place) & (lane < place + 3 * count)
    out_ref[:, cut:] = jnp.where(special, line[0:1], tail).astype(bf16)


def pair_sum(keep, came, kernel=pair_kernel, small=()):
    return pl.pallas_call(
        kernel,
        out_shape=jax.ShapeDtypeStruct(keep.shape, keep.dtype),
        in_specs=[VMEM] * (len(small) + 2),
        out_specs=VMEM,
        compiler_params=pltpu.CompilerParams(vmem_limit_bytes=VMEM_LIMIT // 3),
        name="pair",
    )(*small, keep, came)


def finish_kernel(
    acts, came_ref, in_ref, one_ref, up_ref, two_ref, head_ref, std_ref, loss_ref
):
    ff = up_ref.shape[1]
    obs = in_ref.shape[1]
    heads = head_ref.shape[1]
    total = came_ref[0].astype(jnp.float32)
    for chip in range(1, came_ref.shape[0]):
        total = total + came_ref[chip].astype(jnp.float32)
    up_ref[...] = total[:, :ff]
    in_ref[...] = total[:, ff : ff + obs]
    tail = total[:, ff + LANES :]
    head_ref[...] = tail[:, :heads]
    flipped = jnp.transpose(tail)
    one_ref[...] = flipped[heads : heads + 1]
    two_ref[...] = flipped[heads + 1 : heads + 2]
    count = acts + 1
    place = heads + 2
    whole = (
        pltpu.roll(tail, LANES - place, 1)
        + pltpu.roll(tail, LANES - place - count, 1)
        + pltpu.roll(tail, LANES - place - 2 * count, 1)
    )[0:1]
    std_ref[...] = whole[:, :acts]
    loss_ref[...] = whole[:, acts : acts + 1]


def finish(came, ff, obs, heads, acts):
    rows = came.shape[1]
    shapes = ((rows, obs), (1, rows), (rows, ff), (1, rows), (rows, heads), (1, acts), (1, 1))
    return pl.pallas_call(
        lambda *refs: finish_kernel(acts, *refs),
        out_shape=tuple(jax.ShapeDtypeStruct(shape, jnp.float32) for shape in shapes),
        in_specs=[VMEM],
        out_specs=(VMEM,) * 7,
        compiler_params=pltpu.CompilerParams(vmem_limit_bytes=VMEM_LIMIT // 3),
        name="finish",
    )(came)


def lanes_of(*columns):
    filled = sum(c.shape[1] for c in columns)
    gap = jnp.zeros((columns[0].shape[0], LANES - filled), columns[0].dtype)
    return jnp.concatenate(columns + (gap,), axis=1)


def body(
    q_start, v_start, minv, geom_jac, pairs, gap_start, actions, act_map, batch_index,
    w_in, gain_one, w_up, w_down, gain_two, w_head, log_std, old_mu, advantage, returns,
):
    count = lax.axis_size(EVERY)
    chips = count // 2
    rows_up, ff = w_up.shape
    rows_down, width = w_down.shape
    obs = w_in.shape[0]
    heads = w_head.shape[1]
    acts = log_std.shape[0]
    per_peer = batch_index.shape[2]
    tokens = old_mu.shape[0]
    place = jnp.stack([lax.axis_index("c"), lax.axis_index("x")]).astype(jnp.int32)

    packed = pack(
        w_up, w_down, jnp.transpose(w_in), w_head, gain_one.reshape(1, -1), gain_two.reshape(1, -1)
    )
    beside = [packed]
    for step in (1, 2, 3):
        beside.append(lax.ppermute(packed, "x", [((i + step) % 4, i) for i in range(4)]))
    ordered = jnp.concatenate(beside, axis=1)
    weights = lax.all_gather(ordered, ("z", "y", "c"), axis=0, tiled=True)

    picks = batch_index.reshape(1, count * per_peer)
    q_final, v_final, picked = rollout(
        q_start, v_start, minv, geom_jac, pairs, gap_start, actions, act_map, picks
    )
    row_width = picked.shape[1]
    arrived = lax.all_to_all(
        picked.reshape(count, per_peer, row_width), EVERY, split_axis=0, concat_axis=0, tiled=True
    )
    rows = arrived.reshape(tokens, row_width)
    aux = lanes_of(old_mu, advantage[:, None], returns[:, None])
    std = lanes_of(log_std[None])

    factor = loss_scale / (tokens * count)
    keep, send, pre, dsecond, norm_one, down, dhead, totals, gain_rows = forward(
        place, rows, aux, std, weights, ff, acts, factor
    )

    pair = pair_sum(keep, lax.ppermute(send, "c", SWAP))
    pair, dsecond = lax.optimization_barrier((pair, dsecond))
    down_sum = pair.reshape(4, 4, 4, rows_down, width)
    for axis in WIRE:
        down_sum = lax.psum_scatter(down_sum, axis, scatter_dimension=0, tiled=False)
        down_sum = down_sum.astype(jnp.float32)
    other_totals = lax.ppermute(totals, "c", SWAP)
    keep, send = backward(
        heads, place, rows, weights, gain_rows, pre, dsecond, norm_one, down, dhead
    )
    pair = pair_sum(
        keep,
        lax.ppermute(send, "c", SWAP),
        lambda *refs: pair_totals_kernel(heads + 2, acts + 1, rows_up, *refs),
        (totals, other_totals),
    )
    up_came = lax.all_to_all(
        pair.reshape(chips, rows_up, -1), WIRE, split_axis=0, concat_axis=0, tiled=True
    )
    grad_in, grad_one, grad_up, grad_two, grad_head, grad_std, loss = finish(
        up_came, ff, obs, heads, acts
    )
    return (
        q_final,
        v_final,
        jnp.transpose(grad_in),
        grad_one.reshape(-1),
        grad_up,
        down_sum,
        grad_two.reshape(-1),
        grad_head,
        grad_std.reshape(-1),
        loss.reshape(()) / (tokens * count),
    )


def solution(mesh):
    grid = Mesh(mesh.devices.reshape(4, 4, 4, 2), EVERY)
    placed = (
        P(None, EVERY),
        P(None, EVERY),
        P(None, None, EVERY),
        P(None, None, EVERY),
        P(None, None, EVERY),
        P(None, EVERY),
        P(None, None, EVERY),
        P(),
        P(EVERY, None, None),
        P(None, EVERY),
        P(EVERY),
        P(EVERY, None),
        P(EVERY, None),
        P(EVERY),
        P(EVERY, None),
        P(),
        P(EVERY, None),
        P(EVERY),
        P(EVERY),
    )
    return jax.shard_map(
        body,
        mesh=grid,
        in_specs=placed,
        out_specs=(
            P(None, EVERY),
            P(None, EVERY),
            P(None, EVERY),
            P(EVERY),
            P(EVERY, None),
            P(EVERY, None),
            P(EVERY),
            P(EVERY, None),
            P(),
            P(),
        ),
        check_vma=False,
    )
```

```python
import math

import jax
import jax.numpy as jnp
from jax import lax
from jax.experimental import pallas as pl
from jax.experimental.pallas import tpu as pltpu
from jax.sharding import Mesh
from jax.sharding import PartitionSpec as P

EVERY = ("x", "z", "y", "c")
WIRE = ("x", "z", "y")
LANES = 128
SWAP = [(0, 1), (1, 0)]
VMEM_LIMIT = 46 * 1024 * 1024

BINS = 32
ITERS = 8
time_step = 0.02
damping = 0.5
torque = 2.0
baumgarte = 0.2
soft_reg = 0.1
clip_eps = 0.2
value_coef = 0.5
entropy_coef = 0.01
loss_scale = 1024.0

VMEM = pl.BlockSpec(memory_space=pltpu.VMEM)
SMEM = pl.BlockSpec(memory_space=pltpu.SMEM)


def dot(a, b, dims, precision=None):
    return lax.dot_general(
        a, b, (dims, ((), ())), precision=precision, preferred_element_type=jnp.float32
    )


NN = ((1,), (0,))
NT = ((1,), (1,))
TN = ((0,), (0,))


def spread(row, rows):
    return jnp.broadcast_to(row, (rows, row.shape[-1]))


def rollout_kernel(
    q_ref, v_ref, minv_ref, geom_ref, pairs_ref, gap_ref, act_ref, map_ref, picks_ref,
    q_out, v_out, rows_out,
    select, jac, mob, dela, stored,
):
    geoms, dof, envs = geom_ref.shape
    cont = gap_ref.shape[0]
    steps, acts, _ = act_ref.shape

    @pl.loop(0, geoms)
    def _(g):
        first = (pairs_ref[0] == g).astype(jnp.float32)
        select[g] = first - (pairs_ref[1] == g).astype(jnp.float32)

    def by_rows(count, many, depth, left, right, out):
        @pl.loop(0, count // many)
        def _(block):
            sums = [jnp.zeros((cont, envs), jnp.float32) for _ in range(many)]
            for k in range(depth):
                held = right(k)
                for i in range(many):
                    sums[i] = sums[i] + spread(left(k, block * many + i), cont) * held
            for i in range(many):
                out[block * many + i] = sums[i]

    by_rows(dof, 3, geoms, lambda g, d: geom_ref[g, pl.ds(d, 1), :], lambda g: select[g], jac)
    by_rows(dof, 3, dof, lambda k, d: minv_ref[d, pl.ds(k, 1), :], lambda k: jac[k], mob)
    by_rows(cont, 4, dof, lambda d, e: mob[d, pl.ds(e, 1), :], lambda d: jac[d], dela)

    denom = jnp.full((cont, envs), soft_reg, jnp.float32)
    for e in range(cont):
        denom = denom + jnp.abs(dela[e])
    inverse = 1.0 / denom
    gap_rate = baumgarte / time_step
    q_first = q_ref[...]
    gap_first = gap_ref[...] * gap_rate

    def one_step(s, carry):
        q, v, lam = carry
        level = act_ref[s].astype(jnp.float32) * (2.0 / (BINS - 1)) - 1.0
        force = torque * dot(map_ref[...], level, NN, lax.Precision.HIGHEST) - damping * v
        pushed = jnp.zeros_like(v)
        for k in range(dof):
            pushed = pushed + minv_ref[k] * spread(force[k : k + 1], dof)
        vfree = v + time_step * pushed
        drift = vfree + gap_rate * (q - q_first)
        bias = gap_first
        for d in range(dof):
            bias = bias + jac[d] * spread(drift[d : d + 1], cont)

        def sweep(_, lam):
            push = [bias, jnp.zeros_like(bias)]
            for e in range(cont):
                push[e % 2] = push[e % 2] + dela[e] * spread(lam[e : e + 1], cont)
            return jnp.maximum(lam - (push[0] + push[1]) * inverse, 0.0)

        lam = lax.fori_loop(0, ITERS, sweep, lam)
        gained = [jnp.sum(mob[d] * lam, axis=0, keepdims=True) for d in range(dof)]
        v = vfree + jnp.concatenate(gained, axis=0)
        q = q + time_step * v
        stored[s] = jnp.concatenate([q, v, lam, level], axis=0).astype(jnp.bfloat16)
        return q, v, lam

    q, v, _ = lax.fori_loop(
        0, steps, one_step, (q_first, v_ref[...], jnp.zeros((cont, envs), jnp.float32))
    )
    q_out[...] = q
    v_out[...] = v

    picks = picks_ref.shape[1]
    block = 256
    for start in range(0, picks, block):
        wanted = picks_ref[:, start : start + block]
        found = jnp.zeros((stored.shape[1], block), jnp.float32)
        for s in range(steps):
            ids = lax.broadcasted_iota(jnp.int32, (envs, block), 0) + s * envs
            hit = (ids == wanted).astype(jnp.float32).astype(jnp.bfloat16)
            found = found + dot(stored[s], hit, NN)
        rows_out[start : start + block, :] = jnp.transpose(found).astype(jnp.bfloat16)


def rollout(q_start, v_start, minv, geom_jac, pairs, gap_start, actions, act_map, picks):
    geoms, dof, envs = geom_jac.shape
    cont = gap_start.shape[0]
    steps, acts, _ = actions.shape
    row = 2 * dof + cont + acts
    return pl.pallas_call(
        rollout_kernel,
        out_shape=(
            jax.ShapeDtypeStruct((dof, envs), jnp.float32),
            jax.ShapeDtypeStruct((dof, envs), jnp.float32),
            jax.ShapeDtypeStruct((picks.shape[1], row), jnp.bfloat16),
        ),
        in_specs=[VMEM] * 9,
        out_specs=(VMEM,) * 3,
        scratch_shapes=[
            pltpu.VMEM((geoms, cont, envs), jnp.float32),
            pltpu.VMEM((dof, cont, envs), jnp.float32),
            pltpu.VMEM((dof, cont, envs), jnp.float32),
            pltpu.VMEM((cont, cont, envs), jnp.float32),
            pltpu.VMEM((steps, row, envs), jnp.bfloat16),
        ],
        compiler_params=pltpu.CompilerParams(vmem_limit_bytes=VMEM_LIMIT),
        name="rollout",
    )(q_start, v_start, minv, geom_jac, pairs, gap_start, actions, act_map, picks)


TOKEN_BLOCK = 512
HBM = pl.BlockSpec(memory_space=pl.ANY)
GELU_RATE = math.sqrt(2.0 / math.pi)
GELU_CUBE = 0.044715 * GELU_RATE


def mean_square_root(values):
    return lax.rsqrt(jnp.mean(values * values, axis=1, keepdims=True) + 1e-05)


def norm_backward(grad, values, root):
    inner = jnp.mean(grad * values, axis=1, keepdims=True)
    return root * (grad - values * (root * root * inner))


def split_by_core(core, block, rows, keep_ref, send_ref, start, lane):
    count, columns = block.shape
    groups = block.reshape(count // (2 * rows), 2, rows, columns)
    half = count // 2
    at = pl.ds(pl.multiple_of(start, half), half)
    lanes = slice(lane, lane + columns)
    for which in range(2):
        part = groups[:, which].reshape(half, columns).astype(jnp.bfloat16)

        @pl.when(core == which)
        def _():
            keep_ref[at, lanes] = part

        @pl.when(core != which)
        def _():
            send_ref[at, lanes] = part


def pack_kernel(up_ref, down_ref, in_ref, head_ref, one_ref, two_ref, out_ref):
    rows, ff = up_ref.shape
    width = down_ref.shape[1]
    obs = in_ref.shape[1]
    heads = head_ref.shape[1]
    f32 = jnp.float32
    out_ref[:, :ff] = up_ref[...]
    down = down_ref[...].astype(f32)
    out_ref[:, ff : ff + width] = down[:rows].astype(jnp.bfloat16)
    out_ref[:, ff + width : ff + 2 * width] = down[rows:].astype(jnp.bfloat16)
    first = jnp.concatenate(
        [in_ref[...].astype(f32), jnp.zeros((rows, LANES - obs), f32)], axis=1
    )
    gains = jnp.concatenate(
        [one_ref[...].astype(f32), two_ref[...].astype(f32), jnp.zeros((LANES - 2, rows), f32)],
        axis=0,
    )
    second = pltpu.roll(jnp.transpose(gains), heads, 1)
    wide = jnp.concatenate(
        [head_ref[...].astype(f32), jnp.zeros((rows, LANES - heads), f32)], axis=1
    )
    both = jnp.concatenate([first, second + wide], axis=1)
    out_ref[:, ff + 2 * width :] = both.astype(jnp.bfloat16)


def pack(w_up, w_down, w_in, w_head, gain_one, gain_two):
    rows, ff = w_up.shape
    width = w_down.shape[1]
    return pl.pallas_call(
        pack_kernel,
        out_shape=jax.ShapeDtypeStruct((rows, ff + 2 * width + 2 * LANES), jnp.bfloat16),
        in_specs=[VMEM] * 6,
        out_specs=VMEM,
        name="pack",
    )(w_up, w_down, w_in, w_head, gain_one, gain_two)


def columns_in(weights_ref, parts, first, start, out_ref, sem):
    rows, total = weights_ref.shape
    columns = out_ref.shape[1]
    each = total // parts
    return [
        pltpu.make_async_copy(
            weights_ref.at[:, pl.ds(part * each + start, columns)],
            out_ref.at[pl.ds(pl.multiple_of((first + part) % parts * rows, rows), rows), :],
            sem.at[part],
        )
        for part in range(parts)
    ]


def forward_kernel(
    acts, factor, parts,
    place_ref, rows_ref, aux_ref, std_ref, weights_ref,
    keep_ref, send_hbm, pre_hbm, dsecond_hbm, norm_hbm, down_hbm, dhead_ref, totals_ref, gains_ref,
    up_ref, both_ref, small_ref, down_ref, hidden_ref, pre_ref, dsecond_ref, norm_ref, send_ref,
    in_sem, out_sem,
):
    tokens = rows_ref.shape[0]
    width, ff = up_ref.shape
    load_small = columns_in(weights_ref, parts, place_ref[1], ff + 2 * width, small_ref, in_sem.at[0])
    load_up = columns_in(weights_ref, parts, place_ref[1], 0, up_ref, in_sem.at[1])
    load_both = columns_in(weights_ref, parts, place_ref[1], ff, both_ref, in_sem.at[2])
    for copy in load_small + load_both + load_up:
        copy.start()

    inv_std = jnp.exp(-std_ref[...])
    lane = lax.broadcasted_iota(jnp.int32, (1, LANES), 1)
    is_act = lane < acts
    entropy = jnp.sum(jnp.where(is_act, std_ref[...], 0.0)) + 0.5 * acts * (
        1.0 + math.log(2.0 * math.pi)
    )
    dhead_ref[...] = jnp.zeros_like(dhead_ref)
    totals_ref[...] = jnp.zeros_like(totals_ref)
    low, high = 1.0 - clip_eps, 1.0 + clip_eps

    for copy in load_small:
        copy.wait()
    gains_ref[...] = jnp.transpose(small_ref[:, LANES:].astype(jnp.float32))[acts + 1 : acts + 9]
    gain_one = gains_ref[0:1, :]
    gain_two = gains_ref[1:2, :]

    many = 128
    for part, copy in enumerate(load_both):
        copy.wait()

        @pl.loop(0, width // parts // many)
        def _(step):
            block = (place_ref[1] + part) % parts * (width // parts // many) + step
            at = pl.ds(pl.multiple_of(block * many, many), many)
            halves = both_ref[at, :].astype(jnp.float32).reshape(many // 8, 8, 2 * width)
            mixed = jnp.stack([halves[:, :, :width], halves[:, :, width:]], axis=1)
            to = pl.ds(pl.multiple_of(block * 2 * many, 2 * many), 2 * many)
            down_ref[to, :] = mixed.reshape(2 * many, width).astype(jnp.bfloat16)

    down_out = pltpu.make_async_copy(down_ref, down_hbm, out_sem.at[0])
    down_out.start()
    for copy in load_up:
        copy.wait()

    @pl.loop(0, tokens // TOKEN_BLOCK)
    def _(block):
        at = pl.ds(pl.multiple_of(block * TOKEN_BLOCK, TOKEN_BLOCK), TOKEN_BLOCK)
        rows = rows_ref[at, :]
        first = dot(rows, small_ref[:, :LANES], NT)
        norm_one = (first * mean_square_root(first) * gain_one).astype(jnp.bfloat16)
        norm_ref[at, :] = norm_one
        second = first
        chunk = 1024
        for start in range(0, ff, chunk):
            lanes = slice(start, start + chunk)
            pre = dot(norm_one, up_ref[:, lanes], NN)
            pre_ref[at, lanes] = pre.astype(jnp.bfloat16)
            bent = jnp.tanh(pre * (GELU_RATE + GELU_CUBE * (pre * pre)))
            half = 0.5 * pre
            hidden = (half + half * bent).astype(jnp.bfloat16)
            hidden_ref[at, lanes] = hidden
            second = second + dot(hidden, down_ref[lanes, :], NN)
        pltpu.make_async_copy(pre_ref.at[at, :], pre_hbm.at[at, :], out_sem.at[1]).start()
        pltpu.make_async_copy(norm_ref.at[at, :], norm_hbm.at[at, :], out_sem.at[2]).start()
        root_two = mean_square_root(second)
        scaled = second * root_two
        norm_two = (scaled * gain_two).astype(jnp.bfloat16)
        head = dot(norm_two, small_ref[:, LANES:], NN)

        aux = aux_ref[at, :]
        advantage = aux[:, acts : acts + 1]
        returns = aux[:, acts + 1 : acts + 2]
        taken = pltpu.roll(rows.astype(jnp.float32), acts, 1)
        from_old = jnp.where(is_act, (taken - aux) * inv_std, 0.0)
        from_new = jnp.where(is_act, (taken - head) * inv_std, 0.0)
        apart = from_old * from_old - from_new * from_new
        ratio = jnp.exp(0.5 * jnp.sum(apart, axis=1, keepdims=True))
        free = ratio * advantage
        held = jnp.clip(ratio, low, high) * advantage
        missed = head[:, acts : acts + 1] - returns
        losses = (
            -jnp.minimum(free, held)
            + (0.5 * value_coef) * missed * missed
            - entropy_coef * entropy
        )
        on_free = jnp.where(free < held, 1.0, jnp.where(free == held, 0.5, 0.0))
        inside = jnp.where(
            (ratio > low) & (ratio < high),
            1.0,
            jnp.where((ratio == low) | (ratio == high), 0.5, 0.0),
        )
        dratio = -advantage * (on_free + (1.0 - on_free) * inside)
        dlog = (factor * dratio) * ratio
        dhead = jnp.where(
            is_act,
            dlog * (from_new * inv_std),
            jnp.where(lane == acts, (factor * value_coef) * missed, 0.0),
        )
        dstd = jnp.where(is_act, -dlog * apart - factor * entropy_coef, 0.0)
        both = jnp.where(lane == acts, losses, dstd)
        totals_ref[...] += jnp.sum(both, axis=0, keepdims=True)

        dhead = dhead.astype(jnp.bfloat16)
        dnorm = dot(dhead, small_ref[:, LANES:], NT)
        dhead_ref[0:LANES, :] += dot(dhead, norm_two, TN)
        dhead_ref[LANES : LANES + 1, :] += jnp.sum(dnorm * scaled, axis=0, keepdims=True)
        dsecond = norm_backward(dnorm * gain_two, second, root_two)
        dsecond_ref[at, :] = dsecond.astype(jnp.bfloat16)
        pltpu.make_async_copy(dsecond_ref.at[at, :], dsecond_hbm.at[at, :], out_sem.at[3]).start()

    chunk = 512

    @pl.loop(0, ff // chunk)
    def _(block):
        lanes = pl.ds(pl.multiple_of(block * chunk, chunk), chunk)
        grad = dot(hidden_ref[:, lanes], dsecond_ref[...], TN)
        start = block * (chunk // 2)
        split_by_core(place_ref[0], grad, 16, keep_ref, send_ref, start, 0)
        at = pl.ds(pl.multiple_of(start, chunk // 2), chunk // 2)
        pltpu.make_async_copy(send_ref.at[at, :], send_hbm.at[at, :], out_sem.at[4]).start()

    down_out.wait()
    outs = ((pre_ref, pre_hbm), (norm_ref, norm_hbm), (dsecond_ref, dsecond_hbm))
    for place, (here, there) in enumerate(outs + ((send_ref, send_hbm),)):
        pltpu.make_async_copy(here, there, out_sem.at[place + 1]).wait()


def forward(place, rows, aux, std, weights, ff, acts, factor):
    tokens = rows.shape[0]
    group, total = weights.shape
    width = 1024
    parts = width // group
    bf16, f32 = jnp.bfloat16, jnp.float32
    shapes = [(ff // 2, width), (ff // 2, width), (tokens, ff), (tokens, width), (tokens, width), (ff, width)]
    return pl.pallas_call(
        lambda *refs: forward_kernel(acts, factor, parts, *refs),
        out_shape=tuple(jax.ShapeDtypeStruct(shape, bf16) for shape in shapes)
        + (
            jax.ShapeDtypeStruct((LANES + 8, width), f32),
            jax.ShapeDtypeStruct((1, LANES), f32),
            jax.ShapeDtypeStruct((8, width), f32),
        ),
        in_specs=[SMEM] + [VMEM] * 3 + [HBM],
        out_specs=(VMEM,) + (HBM,) * 5 + (VMEM,) * 3,
        scratch_shapes=[
            pltpu.VMEM((width, ff), bf16),
            pltpu.VMEM((width, 2 * width), bf16),
            pltpu.VMEM((width, 2 * LANES), bf16),
            pltpu.VMEM((ff, width), bf16),
            pltpu.VMEM((tokens, ff), bf16),
            pltpu.VMEM((tokens, ff), bf16),
            pltpu.VMEM((tokens, width), bf16),
            pltpu.VMEM((tokens, width), bf16),
            pltpu.VMEM((ff // 2, width), bf16),
            pltpu.SemaphoreType.DMA((3, parts)),
            pltpu.SemaphoreType.DMA((5,)),
        ],
        compiler_params=pltpu.CompilerParams(vmem_limit_bytes=VMEM_LIMIT),
        cost_estimate=pl.CostEstimate(
            flops=6 * tokens * width * ff, bytes_accessed=30 << 20, transcendentals=tokens * ff
        ),
        name="forward",
    )(place, rows, aux, std, weights)


def backward_up_kernel(
    place_ref, pre_hbm, dsecond_hbm, norm_hbm, down_hbm, dpre_ref, keep_ref, send_hbm,
    pre_ref, dsecond_ref, norm_ref, down_ref, send_ref, in_sem, out_sem,
):
    tokens, ff = pre_ref.shape
    width = norm_ref.shape[1]
    pairs = ((dsecond_hbm, dsecond_ref), (down_hbm, down_ref), (pre_hbm, pre_ref), (norm_hbm, norm_ref))
    loads = [
        pltpu.make_async_copy(there, here, in_sem.at[which])
        for which, (there, here) in enumerate(pairs)
    ]
    for copy in loads:
        copy.start()
    for copy in loads[:3]:
        copy.wait()

    @pl.loop(0, tokens // TOKEN_BLOCK)
    def _(block):
        at = pl.ds(pl.multiple_of(block * TOKEN_BLOCK, TOKEN_BLOCK), TOKEN_BLOCK)
        dsecond = dsecond_ref[at, :]
        chunk = 1024
        for start in range(0, ff, chunk):
            lanes = slice(start, start + chunk)
            dhidden = dot(dsecond, down_ref[lanes, :], NT)
            pre = pre_ref[at, lanes].astype(jnp.float32)
            square = pre * pre
            bent = jnp.tanh(pre * (GELU_RATE + GELU_CUBE * square))
            half = 0.5 * pre
            slope = 0.5 + 0.5 * bent + (half - half * (bent * bent)) * (
                GELU_RATE + (3.0 * GELU_CUBE) * square
            )
            dpre_ref[at, lanes] = (dhidden * slope).astype(jnp.bfloat16)

    loads[3].wait()
    chunk = 512

    @pl.loop(0, width // chunk)
    def _(block):
        lanes = pl.ds(pl.multiple_of(block * chunk, chunk), chunk)
        half = block * (chunk // 2)
        for start in range(0, ff, 1024):
            grad = dot(norm_ref[:, lanes], dpre_ref[:, start : start + 1024], TN)
            split_by_core(place_ref[0], grad, 8, keep_ref, send_ref, half, start)
        at = pl.ds(pl.multiple_of(half, chunk // 2), chunk // 2)
        pltpu.make_async_copy(send_ref.at[at, :], send_hbm.at[at, :], out_sem).start()

    pltpu.make_async_copy(send_ref, send_hbm, out_sem).wait()


def backward_up(place, pre, dsecond, norm_one, down):
    tokens, ff = pre.shape
    width = dsecond.shape[1]
    bf16 = jnp.bfloat16
    out = jax.ShapeDtypeStruct((width // 2, ff), bf16)
    return pl.pallas_call(
        backward_up_kernel,
        out_shape=(jax.ShapeDtypeStruct((tokens, ff), bf16), out, out),
        in_specs=[SMEM] + [HBM] * 4,
        out_specs=(VMEM, VMEM, HBM),
        scratch_shapes=[
            pltpu.VMEM((tokens, ff), bf16),
            pltpu.VMEM((tokens, width), bf16),
            pltpu.VMEM((tokens, width), bf16),
            pltpu.VMEM((ff, width), bf16),
            pltpu.VMEM(out.shape, bf16),
            pltpu.SemaphoreType.DMA((4,)),
            pltpu.SemaphoreType.DMA,
        ],
        compiler_params=pltpu.CompilerParams(vmem_limit_bytes=VMEM_LIMIT),
        cost_estimate=pl.CostEstimate(
            flops=4 * tokens * width * ff, bytes_accessed=20 << 20, transcendentals=tokens * ff
        ),
        name="backward_up",
    )(place, pre, dsecond, norm_one, down)


def backward_in_kernel(
    heads, parts,
    place_ref, rows_ref, weights_ref, gains_ref, dpre_ref, dsecond_ref, dhead_ref,
    keep_ref, send_ref,
    up_ref, win_ref, din_ref, dgain_ref, in_sem,
):
    tokens = rows_ref.shape[0]
    width, ff = up_ref.shape
    load_win = columns_in(weights_ref, parts, place_ref[1], ff + 2 * width, win_ref, in_sem.at[0])
    load_up = columns_in(weights_ref, parts, place_ref[1], 0, up_ref, in_sem.at[1])
    for copy in load_win + load_up:
        copy.start()
    gain_one = gains_ref[0:1, :]
    din_ref[...] = jnp.zeros_like(din_ref)
    dgain_ref[...] = jnp.zeros_like(dgain_ref)
    for copy in load_win + load_up:
        copy.wait()

    @pl.loop(0, tokens // TOKEN_BLOCK)
    def _(block):
        at = pl.ds(pl.multiple_of(block * TOKEN_BLOCK, TOKEN_BLOCK), TOKEN_BLOCK)
        rows = rows_ref[at, :]
        first = dot(rows, win_ref[...], NT)
        root = mean_square_root(first)
        dnorm = dot(dpre_ref[at, :], up_ref[...], NT)
        dgain_ref[0:1, :] += jnp.sum(dnorm * (first * root), axis=0, keepdims=True)
        dfirst = dsecond_ref[at, :].astype(jnp.float32)
        dfirst = dfirst + norm_backward(dnorm * gain_one, first, root)
        din_ref[...] += dot(rows, dfirst.astype(jnp.bfloat16), TN)

    chunk = 512
    ids = lax.broadcasted_iota(jnp.int32, (LANES, chunk), 0)

    @pl.loop(0, width // chunk)
    def _(block):
        lanes = pl.ds(pl.multiple_of(block * chunk, chunk), chunk)
        half = block * (chunk // 2)
        core = place_ref[0]
        split_by_core(core, jnp.transpose(din_ref[:, lanes]), 8, keep_ref, send_ref, half, 0)
        tail = jnp.where(ids == heads, dgain_ref[0:1, lanes], dhead_ref[0:LANES, lanes])
        tail = jnp.where(ids == heads + 1, dhead_ref[LANES : LANES + 1, lanes], tail)
        split_by_core(core, jnp.transpose(tail), 8, keep_ref, send_ref, half, LANES)


def backward_in(heads, place, rows, weights, gains, dpre, dsecond, dhead):
    tokens, ff = dpre.shape
    width = dsecond.shape[1]
    parts = width // weights.shape[0]
    bf16, f32 = jnp.bfloat16, jnp.float32
    out = jax.ShapeDtypeStruct((width // 2, 2 * LANES), bf16)
    return pl.pallas_call(
        lambda *refs: backward_in_kernel(heads, parts, *refs),
        out_shape=(out, out),
        in_specs=[SMEM, VMEM, HBM] + [VMEM] * 4,
        out_specs=(VMEM, VMEM),
        scratch_shapes=[
            pltpu.VMEM((width, ff), bf16),
            pltpu.VMEM((width, LANES), bf16),
            pltpu.VMEM((LANES, width), f32),
            pltpu.VMEM((8, width), f32),
            pltpu.SemaphoreType.DMA((2, parts)),
        ],
        compiler_params=pltpu.CompilerParams(vmem_limit_bytes=VMEM_LIMIT),
        cost_estimate=pl.CostEstimate(
            flops=2 * tokens * width * ff, bytes_accessed=12 << 20, transcendentals=0
        ),
        name="backward_in",
    )(place, rows, weights, gains, dpre, dsecond, dhead)


def pair_kernel(keep_ref, came_ref, out_ref):
    many = keep_ref.shape[0] // 4

    @pl.loop(0, 4)
    def _(block):
        at = pl.ds(pl.multiple_of(block * many, many), many)
        total = keep_ref[at, :].astype(jnp.float32) + came_ref[at, :].astype(jnp.float32)
        out_ref[at, :] = total.astype(jnp.bfloat16)


def pair_totals_kernel(place, count, rows, mine_ref, other_ref, keep_in, came_in, keep_ref, came_ref, out_ref):
    f32, bf16 = jnp.float32, jnp.bfloat16
    ff = keep_ref.shape[1]
    cut = ff + LANES
    pair_kernel(keep_ref, came_ref, out_ref.at[:, :ff])
    pair_kernel(keep_in.at[:, :LANES], came_in.at[:, :LANES], out_ref.at[:, ff:cut])
    lane = lax.broadcasted_iota(jnp.int32, (8, LANES), 1)
    totals = jnp.broadcast_to(mine_ref[...] + other_ref[...], (8, LANES))
    totals = jnp.where(lane < count, totals, 0.0)
    first = totals.astype(bf16).astype(f32)
    second = (totals - first).astype(bf16).astype(f32)
    third = totals - first - second
    line = (
        pltpu.roll(first, place, 1)
        + pltpu.roll(second, place + count, 1)
        + pltpu.roll(third, place + 2 * count, 1)
    )
    tail = keep_in[:, LANES:].astype(f32) + came_in[:, LANES:].astype(f32)
    row = lax.broadcasted_iota(jnp.int32, tail.shape, 0) % rows
    lane = lax.broadcasted_iota(jnp.int32, tail.shape, 1)
    special = (row == 0) & (lane >= place) & (lane < place + 3 * count)
    out_ref[:, cut:] = jnp.where(special, line[0:1], tail).astype(bf16)


def pair_sum(keep, came, kernel=pair_kernel, small=(), more=0):
    return pl.pallas_call(
        kernel,
        out_shape=jax.ShapeDtypeStruct((keep.shape[0], keep.shape[1] + more), keep.dtype),
        in_specs=[VMEM] * (len(small) + 2),
        out_specs=VMEM,
        compiler_params=pltpu.CompilerParams(vmem_limit_bytes=VMEM_LIMIT // 3),
        name="pair",
    )(*small, keep, came)


def finish_kernel(
    acts, came_ref, in_ref, one_ref, up_ref, two_ref, head_ref, std_ref, loss_ref
):
    ff = up_ref.shape[1]
    obs = in_ref.shape[1]
    heads = head_ref.shape[1]
    total = came_ref[0].astype(jnp.float32)
    for chip in range(1, came_ref.shape[0]):
        total = total + came_ref[chip].astype(jnp.float32)
    up_ref[...] = total[:, :ff]
    in_ref[...] = total[:, ff : ff + obs]
    tail = total[:, ff + LANES :]
    head_ref[...] = tail[:, :heads]
    flipped = jnp.transpose(tail)
    one_ref[...] = flipped[heads : heads + 1]
    two_ref[...] = flipped[heads + 1 : heads + 2]
    count = acts + 1
    place = heads + 2
    whole = (
        pltpu.roll(tail, LANES - place, 1)
        + pltpu.roll(tail, LANES - place - count, 1)
        + pltpu.roll(tail, LANES - place - 2 * count, 1)
    )[0:1]
    std_ref[...] = whole[:, :acts]
    loss_ref[...] = whole[:, acts : acts + 1]


def finish(came, ff, obs, heads, acts):
    rows = came.shape[1]
    shapes = ((rows, obs), (1, rows), (rows, ff), (1, rows), (rows, heads), (1, acts), (1, 1))
    return pl.pallas_call(
        lambda *refs: finish_kernel(acts, *refs),
        out_shape=tuple(jax.ShapeDtypeStruct(shape, jnp.float32) for shape in shapes),
        in_specs=[VMEM],
        out_specs=(VMEM,) * 7,
        compiler_params=pltpu.CompilerParams(vmem_limit_bytes=VMEM_LIMIT // 3),
        name="finish",
    )(came)


def lanes_of(*columns):
    filled = sum(c.shape[1] for c in columns)
    gap = jnp.zeros((columns[0].shape[0], LANES - filled), columns[0].dtype)
    return jnp.concatenate(columns + (gap,), axis=1)


def body(
    q_start, v_start, minv, geom_jac, pairs, gap_start, actions, act_map, batch_index,
    w_in, gain_one, w_up, w_down, gain_two, w_head, log_std, old_mu, advantage, returns,
):
    count = lax.axis_size(EVERY)
    chips = count // 2
    rows_up, ff = w_up.shape
    rows_down, width = w_down.shape
    obs = w_in.shape[0]
    heads = w_head.shape[1]
    acts = log_std.shape[0]
    per_peer = batch_index.shape[2]
    tokens = old_mu.shape[0]
    place = jnp.stack([lax.axis_index("c"), lax.axis_index("x")]).astype(jnp.int32)

    packed = pack(
        w_up, w_down, jnp.transpose(w_in), w_head, gain_one.reshape(1, -1), gain_two.reshape(1, -1)
    )
    beside = [packed]
    for step in (1, 2, 3):
        beside.append(lax.ppermute(packed, "x", [((i + step) % 4, i) for i in range(4)]))
    ordered = jnp.concatenate(beside, axis=1)
    weights = lax.all_gather(ordered, ("z", "y", "c"), axis=0, tiled=True)

    picks = batch_index.reshape(1, count * per_peer)
    q_final, v_final, picked = rollout(
        q_start, v_start, minv, geom_jac, pairs, gap_start, actions, act_map, picks
    )
    row_width = picked.shape[1]
    arrived = lax.all_to_all(
        picked.reshape(count, per_peer, row_width), EVERY, split_axis=0, concat_axis=0, tiled=True
    )
    rows = arrived.reshape(tokens, row_width)
    aux = lanes_of(old_mu, advantage[:, None], returns[:, None])
    std = lanes_of(log_std[None])

    factor = loss_scale / (tokens * count)
    keep, send, pre, dsecond, norm_one, down, dhead, totals, gain_rows = forward(
        place, rows, aux, std, weights, ff, acts, factor
    )

    pair = pair_sum(keep, lax.ppermute(send, "c", SWAP))
    pair, dsecond = lax.optimization_barrier((pair, dsecond))
    down_came = lax.all_to_all(
        pair.reshape(chips, rows_down, width), WIRE, split_axis=0, concat_axis=0, tiled=True
    )
    other_totals = lax.ppermute(totals, "c", SWAP)
    dpre, keep, send = backward_up(place, pre, dsecond, norm_one, down)
    came = lax.ppermute(send, "c", SWAP)
    keep_in, send_in = backward_in(
        heads, place, rows, weights, gain_rows, dpre, dsecond, dhead
    )
    send_in, down_came = lax.optimization_barrier((send_in, down_came))
    grad_down = jnp.sum(down_came.astype(jnp.float32), axis=0)
    pair = pair_sum(
        keep,
        came,
        lambda *refs: pair_totals_kernel(heads + 2, acts + 1, rows_up, *refs),
        (totals, other_totals, keep_in, lax.ppermute(send_in, "c", SWAP)),
        2 * LANES,
    )
    up_came = lax.all_to_all(
        pair.reshape(chips, rows_up, -1), WIRE, split_axis=0, concat_axis=0, tiled=True
    )
    grad_in, grad_one, grad_up, grad_two, grad_head, grad_std, loss = finish(
        up_came, ff, obs, heads, acts
    )
    return (
        q_final,
        v_final,
        jnp.transpose(grad_in),
        grad_one.reshape(-1),
        grad_up,
        grad_down,
        grad_two.reshape(-1),
        grad_head,
        grad_std.reshape(-1),
        loss.reshape(()) / (tokens * count),
    )


def solution(mesh):
    grid = Mesh(mesh.devices.reshape(4, 4, 4, 2), EVERY)
    placed = (
        P(None, EVERY),
        P(None, EVERY),
        P(None, None, EVERY),
        P(None, None, EVERY),
        P(None, None, EVERY),
        P(None, EVERY),
        P(None, None, EVERY),
        P(),
        P(EVERY, None, None),
        P(None, EVERY),
        P(EVERY),
        P(EVERY, None),
        P(EVERY, None),
        P(EVERY),
        P(EVERY, None),
        P(),
        P(EVERY, None),
        P(EVERY),
        P(EVERY),
    )
    return jax.shard_map(
        body,
        mesh=grid,
        in_specs=placed,
        out_specs=(
            P(None, EVERY),
            P(None, EVERY),
            P(None, EVERY),
            P(EVERY),
            P(EVERY, None),
            P(EVERY, None),
            P(EVERY),
            P(EVERY, None),
            P(),
            P(),
        ),
        check_vma=False,
    )
```
